256 devices in a mesh: corpus: 64 (over z, y, core), pre: 4 (over x).
Axes of the slice: x: 4, y: 4, z: 8, core: 2. Of those that a mesh axis runs over, the one named last changes fastest.
Arguments:
- passages: bfloat16 [4096, 32, 1024], P('corpus'), may hold values from -6 to 6
- query_weight: bfloat16 [1024, 1024], replicated, may hold values from -0.15625 to 0.15625
- kv_weight: bfloat16 [1024, 1024], replicated, may hold values from -0.15625 to 0.15625
- out_weight: bfloat16 [1024, 1024], replicated, may hold values from -1.5 to 1.5
- score_vector: bfloat16 [1024], replicated, may hold values from -0.1875 to 0.1875
- prefix_key_value_state: bfloat16 [64, 2048, 1024], P('corpus', 'pre'), may hold values from -6 to 6
- candidate_owner: int32 [64, 256, 1], P('corpus', 'pre'), may hold values from 0 to 63; in each aligned block of 64 rows (0 to 63, 64 to 127, ..., all dimensions but the last counted through in order) at most 2 rows name the same one
- candidate_row: int32 [64, 256], P('corpus', 'pre'), may hold values from 0 to 63
- candidate_count: int32 [64], P('corpus'), may hold values from 128 to 256, as said below
Outputs:
- scores: float32 [64, 256], P('corpus', 'pre')
The draws below stay inside these ranges and needn't reach their ends.
Inputs may be any that keep to these rules, and one draw needn't show every extreme that they name: `candidate_owner`: of the 64 slots of one query on one index of pre (slots i * 64 to (i + 1) * 64 - 1), at most 2 name the same owner. `candidate_count`: slots from a query's count on are not live.
All inputs are finite; a program needn't handle non-finite values.
Results may differ from the reference program's by a relative error of at most 0.0075.
Values may be sent and summed in bfloat16 or wider, within the bound.
A program may use at most 128 MiB of HBM per device.

```python
import math
import jax
import jax.numpy as jnp
import numpy as np
from jax import lax

MODEL_WIDTH = 1024
QUERY_HEADS = 8
KEY_VALUE_HEADS = 4
HEAD_SIZE = 128
PREFIX_TOKENS = 2048
PL = 32
CAND_DEV = 64
PASS_DEV = 64
QUERY_COUNT = 64
CAND = 256
PASSAGES = 4096
MOST = 2
N_CORPUS = 64


def shared_basis(key):
    return jnp.clip(jax.random.normal(key, (MODEL_WIDTH, KEY_VALUE_HEADS, HEAD_SIZE), jnp.float32), -3.0, 3.0)


def random_noise(key, target_shape):
    return jnp.clip(jax.random.normal(key, target_shape, jnp.float32), -3.0, 3.0)


def draw_kv_weight(key, part):
    rotary_basis = shared_basis(key)
    key = jax.random.fold_in(key, 11)
    first_half, second_half = jax.random.split(key)
    key_portion = (0.8 * rotary_basis + 0.6 * random_noise(first_half, (MODEL_WIDTH, KEY_VALUE_HEADS, HEAD_SIZE))).reshape(MODEL_WIDTH, KEY_VALUE_HEADS * HEAD_SIZE)
    value_portion = random_noise(second_half, (MODEL_WIDTH, KEY_VALUE_HEADS * HEAD_SIZE))
    joined = jnp.concatenate([key_portion, value_portion], axis=1) * MODEL_WIDTH ** (-0.5)
    return jnp.clip(joined, -5.0 * MODEL_WIDTH ** (-0.5), 5.0 * MODEL_WIDTH ** (-0.5)).astype(jnp.bfloat16)


def draw_query_weight(key, part):
    rotary_basis = shared_basis(key)
    key = jax.random.fold_in(key, 12)
    repeated_heads = jnp.repeat(rotary_basis, QUERY_HEADS // KEY_VALUE_HEADS, axis=1)
    joined = (0.8 * repeated_heads + 0.6 * random_noise(key, (MODEL_WIDTH, QUERY_HEADS, HEAD_SIZE))).reshape(MODEL_WIDTH, QUERY_HEADS * HEAD_SIZE) * MODEL_WIDTH ** (-0.5)
    return jnp.clip(joined, -5.0 * MODEL_WIDTH ** (-0.5), 5.0 * MODEL_WIDTH ** (-0.5)).astype(jnp.bfloat16)


def draw_passages(key, part):
    key = jax.random.fold_in(key, 13)
    first_half, second_half = jax.random.split(key, 2)
    common = random_noise(first_half, (PASSAGES, 1, MODEL_WIDTH))
    rows = 0.8 * common + 0.6 * random_noise(second_half, (PASSAGES, PL, MODEL_WIDTH))
    return jnp.clip(rows, -6.0, 6.0).astype(jnp.bfloat16)


def draw_candidate_count(key, part):
    key = jax.random.fold_in(key, 17)
    first_half, second_half, third = jax.random.split(key, 3)
    counts = jax.random.randint(first_half, (QUERY_COUNT,), CAND // 2, CAND + 1)
    full_place = jax.random.randint(second_half, (), 0, QUERY_COUNT)
    low_place = (full_place + jax.random.randint(third, (), 1, QUERY_COUNT)) % QUERY_COUNT
    places = jnp.arange(QUERY_COUNT)
    counts = jnp.where(places == full_place, CAND, counts)
    counts = jnp.where(places == low_place, CAND // 2, counts)
    return counts.astype(jnp.int32)


def touch_ends(values, rng, least, top_value):
    longest = values.shape.index(max(values.shape))
    spots = []
    for shift in (0, 1):
        where = [jax.random.randint(jax.random.fold_in(rng, axis), (), 0, length) for axis, length in enumerate(values.shape)]
        where[longest] = (where[longest] + shift) % values.shape[longest]
        spots.append(tuple(where))
    return values.at[spots[0]].set(least).at[spots[1]].set(top_value)


def shard_levels(own_key, dims, pieces, low, largest):
    factor_of, own = 1.0, jax.random.fold_in(own_key, 6)
    for dim, shards_of in pieces:
        steps = jnp.exp(jax.random.uniform(jax.random.fold_in(own, dim), (shards_of,), jnp.float32, low / len(pieces), largest / len(pieces)))
        factor_of = factor_of * jnp.repeat(steps, dims[dim] // shards_of).reshape([-1 if axis == dim else 1 for axis in range(len(dims))])
    return factor_of


def assign_block(stream_key, own, number, rows, number_of, top, limit, slope):
    sequence = jax.random.permutation(stream_key, number_of)
    heavy_load, usual = portions_of(number_of, rows * top, limit, slope, True), portions_of(number_of, rows * top, limit, slope, False)
    places = jnp.arange(number_of)

    def named(tallies, offset_by):
        used = int((tallies > 0).sum())
        fixed = max(1, used // 4)
        moved = fixed + (places - fixed + offset_by * (used - fixed)) % max(1, number_of - fixed)
        return jnp.zeros((number_of,), jnp.int32).at[sequence[jnp.where(places < fixed, places, moved)]].set(jnp.asarray(tallies, jnp.int32))

    tallies = jnp.where(number % 4 == 0, named(heavy_load, number // 4), named(usual, number - number // 4 - 1))
    mixed = jax.random.permutation(jax.random.fold_in(own, 3), number_of)
    source_of, taker = mixed[0:number_of // 2 * 2:2], mixed[1:number_of // 2 * 2:2]
    margin = jnp.minimum(tallies[source_of] - 1, limit - tallies[taker]) // 2
    margin = jnp.where((source_of == sequence[0]) | (taker == sequence[0]) | (tallies[taker] == 0), 0, jnp.maximum(margin, 0))
    moved = jax.random.randint(jax.random.fold_in(own, 4), (number_of // 2,), 0, 1 << 20) % (margin + 1)
    tallies = tallies.at[source_of].add(-moved).at[taker].add(moved)
    labels = jnp.searchsorted(jnp.cumsum(tallies), jnp.arange(rows * top), side="right").astype(jnp.int32)
    grid = labels.reshape(top, rows).T
    grid = grid[jax.random.permutation(jax.random.fold_in(own, 1), rows)]
    offset_by = jax.random.randint(jax.random.fold_in(own, 2), (rows, 1), 0, top)
    return jnp.take_along_axis(grid, (jnp.arange(top)[None, :] + offset_by) % top, axis=1)


def portions_of(amount, total, limit, lean, full):
    portions = [(1 << 20) // math.isqrt(grade ** lean) + 1 for grade in range(1, amount + 1)]
    largest = limit if full else min(limit, max(-(-total // amount), total * portions[0] // sum(portions)))
    least = 1 if total - largest >= amount - 1 else 0
    given, surplus = [largest] + [least] * (amount - 1), total - largest - least * (amount - 1)
    while surplus > 0:
        free = [i for i in range(1, amount) if given[i] < largest] or [i for i in range(1, amount) if given[i] < limit]
        whole, left = sum([portions[i] for i in free]), surplus
        for i in free:
            addition = min(limit - given[i], max(1, left * portions[i] // whole), surplus)
            given[i] = given[i] + addition
            surplus = surplus - addition
    return np.array(given)


def bell_draw(key, extent, scale, bound, cuts=(), kind=jnp.bfloat16):
    values = scale * jax.random.normal(key, extent, jnp.float32)
    if cuts:
        values = values * shard_levels(key, extent, cuts, -0.22, 0.18)
    return jnp.clip(values, -bound, bound).astype(kind)


def setup_inputs(seed: int = 0) -> dict:
    seeds = jax.random.split(jax.random.key(seed), 10)
    passages = draw_passages(jax.random.fold_in(seeds[9], 71), 0)
    query_weight = draw_query_weight(jax.random.fold_in(seeds[9], 71), 0)
    kv_weight = draw_kv_weight(jax.random.fold_in(seeds[9], 71), 0)
    out_weight = bell_draw(seeds[3], (QUERY_HEADS * HEAD_SIZE, MODEL_WIDTH), (HEAD_SIZE // 8) ** -0.5, 1.5)
    score_vector = bell_draw(seeds[4], (MODEL_WIDTH,), MODEL_WIDTH ** -0.5, 0.1875)
    prefix_key_value_state = bell_draw(seeds[5], (QUERY_COUNT, PREFIX_TOKENS, 2 * KEY_VALUE_HEADS * HEAD_SIZE), 1.0, 6.0, ((0, 64), (1, 4)))
    candidate_owner_keys = jax.random.split(jax.random.fold_in(seeds[6], 1), QUERY_COUNT * CAND // CAND_DEV)
    candidate_owner_turns = jax.random.permutation(jax.random.fold_in(seeds[6], 3), QUERY_COUNT * CAND // CAND_DEV)
    candidate_owner = jax.vmap(lambda own, number: assign_block(jax.random.fold_in(seeds[6], 2), own, number, CAND_DEV, N_CORPUS, 1, MOST, 2))(candidate_owner_keys, candidate_owner_turns).reshape((QUERY_COUNT, CAND, 1))
    candidate_row = touch_ends(jax.random.randint(seeds[7], (QUERY_COUNT, CAND), 0, PASS_DEV), jax.random.fold_in(seeds[7], 1), 0, PASS_DEV - 1).astype(jnp.int32)
    candidate_count = draw_candidate_count(jax.random.fold_in(seeds[9], 71), 0)
    return dict(passages=passages, query_weight=query_weight, kv_weight=kv_weight, out_weight=out_weight, score_vector=score_vector, prefix_key_value_state=prefix_key_value_state, candidate_owner=candidate_owner, candidate_row=candidate_row, candidate_count=candidate_count)


epsilon = 1e-06
theta_base = 1000000.0

def rms_rows(value_rows):
    return value_rows * lax.rsqrt(lax.optimization_barrier(jnp.mean(value_rows * value_rows, axis=-1, keepdims=True)) + epsilon)

def rotate(value_rows, token_positions):
    half_width = value_rows.shape[-1] // 2
    exponent = jnp.arange(half_width, dtype=jnp.float32) * (2.0 / value_rows.shape[-1])
    angles = token_positions.astype(jnp.float32)[:, None] * (theta_base ** (-exponent))[None, :]
    cosine = jnp.cos(angles)[:, None, :]
    sine = jnp.sin(angles)[:, None, :]
    leading = value_rows[..., :half_width]
    trailing = value_rows[..., half_width:]
    return jnp.concatenate([leading * cosine - trailing * sine, trailing * cosine + leading * sine], axis=-1)

def turned_keys(unrotated_keys, token_positions):
    reshaped_rows = unrotated_keys.reshape(unrotated_keys.shape[:-1] + (KEY_VALUE_HEADS, HEAD_SIZE))
    return rotate(rms_rows(reshaped_rows), token_positions).astype(jnp.bfloat16)

def passage_states(hidden, kv_weight):
    row_tally = hidden.shape[0]
    prefix_length = hidden.shape[1]
    normed = rms_rows(hidden.astype(jnp.float32)).astype(jnp.bfloat16)
    projected_rows = jnp.dot(normed.reshape(row_tally * prefix_length, hidden.shape[2]), kv_weight, preferred_element_type=jnp.float32)
    projected_rows = projected_rows.reshape(row_tally, prefix_length, 2 * KEY_VALUE_HEADS * HEAD_SIZE)
    token_positions = PREFIX_TOKENS + jnp.arange(prefix_length, dtype=jnp.int32)
    key_rows = turned_keys(projected_rows[..., :KEY_VALUE_HEADS * HEAD_SIZE], token_positions)
    value_rows = projected_rows[..., KEY_VALUE_HEADS * HEAD_SIZE:].astype(jnp.bfloat16)
    return (key_rows, value_rows)

def last_query(last_hidden, query_weight):
    normed = rms_rows(last_hidden.astype(jnp.float32)).astype(jnp.bfloat16)
    projected_rows = jnp.dot(normed, query_weight, preferred_element_type=jnp.float32)
    reshaped_rows = projected_rows.reshape(last_hidden.shape[0], 1, QUERY_HEADS, HEAD_SIZE)
    position = jnp.full((1,), PREFIX_TOKENS + PL - 1, jnp.int32)
    return rotate(rms_rows(reshaped_rows), position)[:, 0].astype(jnp.bfloat16)

def prefix_terms(query_rows, block_slice, start_offset):
    prefix_length = block_slice.shape[0]
    key_rows = turned_keys(block_slice[:, :KEY_VALUE_HEADS * HEAD_SIZE].astype(jnp.float32), start_offset + jnp.arange(prefix_length, dtype=jnp.int32))
    value_rows = block_slice[:, KEY_VALUE_HEADS * HEAD_SIZE:].reshape(prefix_length, KEY_VALUE_HEADS, HEAD_SIZE)
    grouped_heads = query_rows.reshape(query_rows.shape[0], KEY_VALUE_HEADS, QUERY_HEADS // KEY_VALUE_HEADS, HEAD_SIZE)
    logits = jnp.einsum('sghd,pgd->sghp', grouped_heads.astype(jnp.float32), key_rows.astype(jnp.float32)) * HEAD_SIZE ** (-0.5)
    expo = jnp.exp(logits)
    rounded = lax.optimization_barrier(expo.astype(jnp.bfloat16))
    weighted = jnp.einsum('sghp,pgd->sghd', rounded.astype(jnp.float32), value_rows.astype(jnp.float32))
    return (weighted, lax.optimization_barrier(jnp.sum(expo, axis=-1)))

def passage_terms(query_rows, key_rows, value_rows):
    row_tally = query_rows.shape[0]
    grouped_heads = query_rows.reshape(row_tally, KEY_VALUE_HEADS, QUERY_HEADS // KEY_VALUE_HEADS, HEAD_SIZE)
    logits = jnp.einsum('sghd,stgd->sght', grouped_heads.astype(jnp.float32), key_rows.astype(jnp.float32)) * HEAD_SIZE ** (-0.5)
    expo = jnp.exp(logits)
    rounded = lax.optimization_barrier(expo.astype(jnp.bfloat16))
    reshaped_values = value_rows.reshape(row_tally, value_rows.shape[1], KEY_VALUE_HEADS, HEAD_SIZE)
    weighted = jnp.einsum('sght,stgd->sghd', rounded.astype(jnp.float32), reshaped_values.astype(jnp.float32))
    return (weighted, lax.optimization_barrier(jnp.sum(expo, axis=-1)))

def finish(weighted, totals, last_hidden, out_weight, score_vector):
    mixed = (weighted / totals[..., None]).reshape(weighted.shape[0], QUERY_HEADS * HEAD_SIZE).astype(jnp.bfloat16)
    output = jnp.dot(mixed, out_weight, preferred_element_type=jnp.float32)
    updated = last_hidden.astype(jnp.float32) + output
    return lax.optimization_barrier(jnp.sum(rms_rows(updated) * score_vector.astype(jnp.float32), axis=-1))

def reference(passages, query_weight, kv_weight, out_weight, score_vector, prefix_key_value_state, candidate_owner, candidate_row, candidate_count):

    def one_query(inputs):
        owners, rows, count, prefix = inputs
        hidden = passages[owners[:, 0] * PASS_DEV + rows]
        key_rows, value_rows = passage_states(hidden, kv_weight)
        query_rows = last_query(hidden[:, -1], query_weight)
        weighted, totals = passage_terms(query_rows, key_rows, value_rows)
        far_weighted, far_totals = prefix_terms(query_rows, prefix, jnp.zeros((), jnp.int32))
        result = finish(weighted + far_weighted, totals + far_totals, hidden[:, -1], out_weight, score_vector)
        live = jnp.arange(CAND, dtype=jnp.int32) < count
        return jnp.where(live, result, jnp.zeros_like(result))
    return lax.map(one_query, (candidate_owner, candidate_row, candidate_count, prefix_key_value_state))
```

```python
import jax
import jax.numpy as jnp
import numpy as np
from jax import lax
from jax.experimental import pallas as pl
from jax.experimental.pallas import tpu as pltpu
from jax.sharding import PartitionSpec as P

MESH = pl.DeviceIdType.MESH
BF = jnp.bfloat16
F32 = jnp.float32

OWNERS = 64
PRE = 4
SLOTS = 64
PASS = 64
TOKENS = 32
WIDTH = 1024
HEADS = 8
GROUPS = 4
HEAD = 128
PREFIX = 2048
SHARE = PREFIX // PRE
CHUNK = 512
CHUNK_PASS = CHUNK // TOKENS
SCALE = HEAD**-0.5
EPS = 1e-06
PART = HEAD + 16


def angle_table():
    half = HEAD // 2
    exponent = np.arange(half, dtype=np.float32) * np.float32(2.0 / HEAD)
    freq = np.float32(1000000.0) ** (-exponent)
    angles = np.arange(PREFIX + TOKENS, dtype=np.float32)[:, None] * freq[None, :]
    angles = angles.astype(np.float64)
    return np.concatenate([np.cos(angles), np.sin(angles)], axis=1).astype(np.float32)


def iota(shape, dim):
    return lax.broadcasted_iota(jnp.int32, shape, dim)


def cos_sin(table):
    swapped = pltpu.roll(table, HEAD // 2, 1)
    low = iota(table.shape, 1) < HEAD // 2
    return jnp.where(low, table, swapped), jnp.where(low, -swapped, table)


def unit(rows):
    return rows * lax.rsqrt(jnp.mean(rows * rows, axis=-1, keepdims=True) + EPS)


def turn(rows, cosine, sine):
    return rows * cosine + pltpu.roll(rows, HEAD // 2, 1) * sine


def dot(a, b):
    return jnp.dot(a, b, preferred_element_type=F32)


def dot_t(a, b):
    return lax.dot_general(a, b, (((1,), (1,)), ((), ())), preferred_element_type=F32)


def split_two(total):
    high = total.astype(BF).astype(F32)
    return high, total - high


def kernel(
    passages, query_weight, kv_weight, out_weight, score_vector, prefix, table,
    owner_col, owner_row, row_row, count, out,
    pas, wq, wkv, wo, pre_v, tab, tail,
    last32, own_rows, own_sums, own_tots, own_query, own_tot,
    pre_keys, req_out, req_in, pick, place,
    last_out, last_in, sums_out, sums_in, query_all, part_out, part_in, slot_last,
    load_sem, send_sem, recv_sem,
):
    me = lax.axis_index("corpus")
    px = lax.axis_index("pre")

    loads = [
        (passages, pas),
        (query_weight, wq),
        (table.at[pl.ds(PREFIX, TOKENS)], tail),
        (prefix, pre_v),
        (table.at[pl.ds(pl.multiple_of(px * SHARE, SHARE), SHARE)], tab),
        (kv_weight, wkv),
        (out_weight, wo),
    ]
    copies = [
        pltpu.make_async_copy(src, dst, load_sem.at[i])
        for i, (src, dst) in enumerate(loads)
    ]

    barrier = pltpu.get_barrier_semaphore()

    def greet(i, carry):
        peer = lax.rem(me + i, OWNERS)
        pl.semaphore_signal(barrier, inc=1, device_id={"corpus": peer}, device_id_type=MESH)
        return carry

    lax.fori_loop(1, OWNERS, greet, 0)
    for k in (2, 1, 3):
        pl.semaphore_signal(
            barrier, inc=1, device_id={"pre": lax.rem(px + k, PRE)}, device_id_type=MESH
        )
    for copy in copies:
        copy.start()

    def spread(source, target, channel):
        def send(i, carry):
            peer = lax.rem(me + i, OWNERS)
            pltpu.make_async_remote_copy(
                src_ref=source.at[peer],
                dst_ref=target.at[me],
                send_sem=send_sem.at[channel],
                recv_sem=recv_sem.at[channel],
                device_id={"corpus": peer},
                device_id_type=MESH,
            ).start()
            return carry

        target[me] = source[me]
        lax.fori_loop(1, OWNERS, send, 0)

    def wait_for(ref, semaphore):
        pltpu.make_async_copy(ref, ref, semaphore).wait()

    owners_c = owner_col[...]
    owners_r = owner_row[...]
    same = owners_c == owners_r
    ia = iota((SLOTS, SLOTS), 0)
    ib = iota((SLOTS, SLOTS), 1)
    rank_r = jnp.sum(jnp.where(same & (ia < ib), 1.0, 0.0), axis=0, keepdims=True)
    rank_c = jnp.sum(jnp.where(same & (ib < ia), 1.0, 0.0), axis=1, keepdims=True)
    mine = jnp.where(ia == owners_r, row_row[...].astype(F32), 0.0)
    first = jnp.sum(jnp.where(rank_r < 0.5, mine, 0.0), axis=1, keepdims=True)
    second = jnp.sum(jnp.where(rank_r > 0.5, mine, 0.0), axis=1, keepdims=True)
    lane = iota((OWNERS, 128), 1)
    message = jnp.where(lane < 8, first, second) + ((lane & 7) * PASS).astype(F32)
    req_out[...] = message.reshape(OWNERS, 1, 128)

    spot = owners_c * 16 + rank_c.astype(jnp.int32) * 8
    for j in range(8):
        place[j * SLOTS : (j + 1) * SLOTS, :] = jnp.where(
            iota((SLOTS, OWNERS * 16), 1) == spot + j, 1.0, 0.0
        ).astype(BF)

    copies[0].wait()

    def take_last(r, carry):
        start = pl.multiple_of(r * TOKENS + 16, 16)
        last32[pl.ds(r, 1), :] = pas[pl.ds(start, 16), :].astype(F32)[15:16, :]
        return carry

    lax.fori_loop(0, PASS, take_last, 0)
    last = last32[...]
    for j in range(8):
        own_rows[j * PASS : (j + 1) * PASS, :] = last[:, j * 128 : (j + 1) * 128].astype(BF)

    copies[1].wait()
    copies[2].wait()
    tail_cos, tail_sin = cos_sin(tail[...])
    end_cos, end_sin = tail_cos[TOKENS - 1 :, :], tail_sin[TOKENS - 1 :, :]

    def query_of(rows32):
        projected = dot(unit(rows32).astype(BF), wq[...])
        return [
            turn(unit(projected[:, h * HEAD : (h + 1) * HEAD]), end_cos, end_sin).astype(BF)
            for h in range(HEADS)
        ]

    for h, rows in enumerate(query_of(last)):
        own_query[h] = rows

    copies[3].wait()
    copies[4].wait()
    for half in range(2):
        span = slice(half * 256, (half + 1) * 256)
        cosine, sine = cos_sin(tab[span, :])
        for g in range(GROUPS):
            rows = pre_v[span, g * HEAD : (g + 1) * HEAD].astype(F32)
            pre_keys[g, span, :] = turn(unit(rows), cosine, sine).astype(BF)

    copies[5].wait()

    def own_chunk(c, carry):
        start = pl.multiple_of(c * CHUNK, CHUNK)
        hidden = pas[pl.ds(start, CHUNK), :]
        hidden32 = hidden.astype(F32)
        factor = lax.rsqrt(jnp.mean(hidden32 * hidden32, axis=-1, keepdims=True) + EPS)
        first_row = pl.multiple_of(c * CHUNK_PASS, CHUNK_PASS)
        cosine = jnp.broadcast_to(tail_cos[None], (CHUNK_PASS, TOKENS, HEAD)).reshape(CHUNK, HEAD)
        sine = jnp.broadcast_to(tail_sin[None], (CHUNK_PASS, TOKENS, HEAD)).reshape(CHUNK, HEAD)
        shape = (2 * CHUNK_PASS, CHUNK)
        own = (iota(shape, 0) % CHUNK_PASS) == (iota(shape, 1) // TOKENS)
        for g in range(GROUPS):
            cols = slice(g * HEAD, (g + 1) * HEAD)
            v_cols = slice((GROUPS + g) * HEAD, (GROUPS + g + 1) * HEAD)
            keys = turn(unit(dot(hidden, wkv[:, cols]) * factor), cosine, sine).astype(BF)
            values = (dot(hidden, wkv[:, v_cols]) * factor).astype(BF)
            queries = jnp.concatenate(
                [own_query[2 * g + i, pl.ds(first_row, CHUNK_PASS), :] for i in range(2)], axis=0
            )
            expo = jnp.where(own, jnp.exp(dot_t(queries, keys) * SCALE), 0.0)
            weighted = dot(expo.astype(BF), values)
            total = jnp.sum(expo, axis=1, keepdims=True)
            for i in range(2):
                rows = slice(i * CHUNK_PASS, (i + 1) * CHUNK_PASS)
                own_sums[2 * g + i, pl.ds(first_row, CHUNK_PASS), :] = weighted[rows].astype(BF)
                own_tot[2 * g + i, pl.ds(first_row, CHUNK_PASS), :] = jnp.broadcast_to(
                    total[rows], (CHUNK_PASS, HEAD)
                )
        return carry

    pl.semaphore_wait(barrier, OWNERS - 1 + PRE - 1)
    spread(req_out, req_in, 0)

    lax.fori_loop(0, PASS // CHUNK_PASS, own_chunk, 0)
    high, low = split_two(own_tot[...])
    own_tots[...] = jnp.where(iota((HEADS, PASS, HEAD), 2) < 64, high, low).astype(BF)

    wait_for(req_in.at[pl.ds(0, OWNERS - 1)], recv_sem.at[0])
    shape = (OWNERS * 16, 128)
    asked = jnp.broadcast_to(req_in[...], (OWNERS, 16, 128)).reshape(shape)
    asked = jnp.where(iota(shape, 1) == (iota(shape, 0) & 15), asked, 0.0)
    asked = jnp.sum(asked, axis=1, keepdims=True).astype(jnp.int32)
    pick[...] = jnp.where(iota((OWNERS * 16, 8 * PASS), 1) == asked, 1.0, 0.0).astype(BF)
    last_out[...] = dot(pick[...], own_rows[...]).astype(BF).reshape(OWNERS, 16, 128)
    spread(last_out, last_in, 1)
    sums_out[:, 0:16, :] = (
        dot(pick[...], own_sums[...].reshape(HEADS * PASS, HEAD)).astype(BF).reshape(OWNERS, 16, 128)
    )
    sums_out[:, 16:32, :] = (
        dot(pick[...], own_tots[...].reshape(HEADS * PASS, HEAD)).astype(BF).reshape(OWNERS, 16, 128)
    )
    spread(sums_out, sums_in, 2)

    wait_for(last_in.at[pl.ds(0, OWNERS - 1)], recv_sem.at[1])
    got = dot(place[...], last_in[...].reshape(OWNERS * 16, 128))
    slot_last[...] = jnp.concatenate(
        [got[j * SLOTS : (j + 1) * SLOTS, :] for j in range(8)], axis=1
    )
    queries = query_of(slot_last[...])
    for g in range(GROUPS):
        query_all[g, px] = jnp.concatenate([queries[2 * g], queries[2 * g + 1]], axis=0)
        for k in (2, 1, 3):
            pltpu.make_async_remote_copy(
                src_ref=query_all.at[g, px],
                dst_ref=query_all.at[g, px],
                send_sem=send_sem.at[3 + g],
                recv_sem=recv_sem.at[3 + g],
                device_id={"pre": lax.rem(px + k, PRE)},
                device_id_type=MESH,
            ).start()

    diagonal = iota((HEAD, HEAD), 0) == iota((HEAD, HEAD), 1)
    for g in range(GROUPS):
        wait_for(query_all.at[g, pl.ds(0, PRE - 1)], recv_sem.at[3 + g])
        values = pre_v[:, (GROUPS + g) * HEAD : (GROUPS + g + 1) * HEAD]
        for q in range(PRE):
            expo = jnp.exp(dot_t(query_all[g, q], pre_keys[g]) * SCALE)
            part_out[g, q, 0:HEAD, :] = dot(expo.astype(BF), values).astype(BF)
            total = jnp.sum(expo, axis=1, keepdims=True)
            total = jnp.sum(jnp.where(diagonal, total, 0.0), axis=0, keepdims=True)
            high, low = split_two(total)
            part_out[g, q, HEAD:PART, :] = jnp.where(
                iota((PART - HEAD, HEAD), 0) == 0, high, low
            ).astype(BF)
        part_in[g, px] = part_out[g, px]
        for k in (2, 1, 3):
            to = lax.rem(px + k, PRE)
            pltpu.make_async_remote_copy(
                src_ref=part_out.at[g, to],
                dst_ref=part_in.at[g, px],
                send_sem=send_sem.at[7 + g],
                recv_sem=recv_sem.at[7 + g],
                device_id={"pre": to},
                device_id_type=MESH,
            ).start()

    wait_for(sums_in.at[pl.ds(0, OWNERS - 1)], recv_sem.at[2])
    own_w = dot(place[...], sums_in[:, 0:16, :].reshape(OWNERS * 16, 128))
    own_t = dot(place[...], sums_in[:, 16:32, :].reshape(OWNERS * 16, 128))
    own_t = own_t[:, 0:1] + own_t[:, 64:65]
    copies[6].wait()
    mixed = []
    for g in range(GROUPS):
        wait_for(part_in.at[g, pl.ds(0, PRE - 1)], recv_sem.at[7 + g])
        rows = slice(g * 2 * SLOTS, (g + 1) * 2 * SLOTS)
        weighted = own_w[rows]
        total = jnp.zeros((1, HEAD), F32)
        for q in range(PRE):
            weighted = weighted + part_in[g, q, 0:HEAD, :].astype(F32)
            sums = part_in[g, q, HEAD:PART, :].astype(F32)
            total = total + sums[0:1, :] + sums[1:2, :]
        total = jnp.sum(jnp.where(diagonal, total, 0.0), axis=1, keepdims=True) + own_t[rows]
        result = (weighted / total).astype(BF)
        mixed += [result[0:SLOTS], result[SLOTS:]]
    updated = slot_last[...] + dot(jnp.concatenate(mixed, axis=1), wo[...])
    square = jnp.mean(updated * updated, axis=-1, keepdims=True)
    score = jnp.sum(updated * score_vector[...].astype(F32), axis=-1, keepdims=True)
    score = score * lax.rsqrt(square + EPS)
    score = jnp.sum(jnp.where(ia == ib, score, 0.0), axis=0, keepdims=True)
    slot = px * SLOTS + iota((1, SLOTS), 1)
    out[...] = jnp.where(slot < count[...], score, 0.0)

    wait_for(req_out.at[pl.ds(0, OWNERS - 1)], send_sem.at[0])
    wait_for(last_out.at[pl.ds(0, OWNERS - 1)], send_sem.at[1])
    wait_for(sums_out.at[pl.ds(0, OWNERS - 1)], send_sem.at[2])
    for g in range(GROUPS):
        wait_for(query_all.at[g, pl.ds(0, PRE - 1)], send_sem.at[3 + g])
        wait_for(part_out.at[g, pl.ds(0, PRE - 1)], send_sem.at[7 + g])


def per_device(
    passages,
    query_weight,
    kv_weight,
    out_weight,
    score_vector,
    prefix,
    candidate_owner,
    candidate_row,
    candidate_count,
):
    hbm = pl.BlockSpec(memory_space=pl.ANY)
    vmem = pl.BlockSpec(memory_space=pltpu.VMEM)
    return pl.pallas_call(
        kernel,
        out_shape=jax.ShapeDtypeStruct((1, SLOTS), F32),
        in_specs=[hbm, hbm, hbm, hbm, vmem, hbm, hbm, vmem, vmem, vmem, vmem],
        out_specs=vmem,
        scratch_shapes=[
            pltpu.VMEM((PASS * TOKENS, WIDTH), BF),
            pltpu.VMEM((WIDTH, WIDTH), BF),
            pltpu.VMEM((WIDTH, WIDTH), BF),
            pltpu.VMEM((WIDTH, WIDTH), BF),
            pltpu.VMEM((SHARE, WIDTH), BF),
            pltpu.VMEM((SHARE, HEAD), F32),
            pltpu.VMEM((TOKENS, HEAD), F32),
            pltpu.VMEM((PASS, WIDTH), F32),
            pltpu.VMEM((8 * PASS, 128), BF),
            pltpu.VMEM((HEADS, PASS, HEAD), BF),
            pltpu.VMEM((HEADS, PASS, HEAD), BF),
            pltpu.VMEM((HEADS, PASS, HEAD), BF),
            pltpu.VMEM((HEADS, PASS, HEAD), F32),
            pltpu.VMEM((GROUPS, SHARE, HEAD), BF),
            pltpu.VMEM((OWNERS, 1, 128), F32),
            pltpu.VMEM((OWNERS, 1, 128), F32),
            pltpu.VMEM((OWNERS * 16, 8 * PASS), BF),
            pltpu.VMEM((8 * SLOTS, OWNERS * 16), BF),
            pltpu.VMEM((OWNERS, 16, 128), BF),
            pltpu.VMEM((OWNERS, 16, 128), BF),
            pltpu.VMEM((OWNERS, 32, 128), BF),
            pltpu.VMEM((OWNERS, 32, 128), BF),
            pltpu.VMEM((GROUPS, PRE, 2 * SLOTS, HEAD), BF),
            pltpu.VMEM((GROUPS, PRE, PART, HEAD), BF),
            pltpu.VMEM((GROUPS, PRE, PART, HEAD), BF),
            pltpu.VMEM((SLOTS, WIDTH), F32),
            pltpu.SemaphoreType.DMA((7,)),
            pltpu.SemaphoreType.DMA((11,)),
            pltpu.SemaphoreType.DMA((11,)),
        ],
        compiler_params=pltpu.CompilerParams(
            collective_id=0, has_side_effects=True, vmem_limit_bytes=48 * 2**20
        ),
        cost_estimate=pl.CostEstimate(
            flops=6 * 10**9, bytes_accessed=12 * 2**20, transcendentals=2 * 10**6
        ),
    )(
        passages.reshape(PASS * TOKENS, WIDTH),
        query_weight,
        kv_weight,
        out_weight,
        score_vector.reshape(1, WIDTH),
        prefix[0],
        jnp.asarray(angle_table()),
        candidate_owner[0],
        candidate_owner.reshape(1, SLOTS),
        candidate_row,
        candidate_count.reshape(1, 1),
    )


def solution(mesh):
    return jax.shard_map(
        per_device,
        mesh=mesh,
        in_specs=(
            P("corpus", None, None),
            P(),
            P(),
            P(),
            P(),
            P("corpus", "pre", None),
            P("corpus", "pre", None),
            P("corpus", "pre"),
            P("corpus"),
        ),
        out_specs=P("corpus", "pre"),
        check_vma=False,
    )
```

```python
import jax
import jax.numpy as jnp
import numpy as np
from jax import lax
from jax.experimental import pallas as pl
from jax.experimental.pallas import tpu as pltpu
from jax.sharding import PartitionSpec as P

MESH = pl.DeviceIdType.MESH
BF = jnp.bfloat16
F32 = jnp.float32

OWNERS = 64
PRE = 4
SLOTS = 64
PASS = 64
TOKENS = 32
WIDTH = 1024
HEADS = 8
GROUPS = 4
HEAD = 128
PREFIX = 2048
SHARE = PREFIX // PRE
CHUNK = 512
SCALE = HEAD**-0.5
EPS = 1e-06
PART = HEAD + 16
VLIM = 62
BLOCK = PASS // PRE
WHOLE = 1


def angle_table():
    half = HEAD // 2
    exponent = np.arange(half, dtype=np.float32) * np.float32(2.0 / HEAD)
    freq = np.float32(1000000.0) ** (-exponent)
    angles = np.arange(PREFIX + TOKENS, dtype=np.float32)[:, None] * freq[None, :]
    angles = angles.astype(np.float64)
    return np.concatenate([np.cos(angles), np.sin(angles)], axis=1).astype(np.float32)


def iota(shape, dim):
    return lax.broadcasted_iota(jnp.int32, shape, dim)


def cos_sin(table):
    swapped = pltpu.roll(table, HEAD // 2, 1)
    low = iota(table.shape, 1) < HEAD // 2
    return jnp.where(low, table, swapped), jnp.where(low, -swapped, table)


def unit(rows):
    return rows * lax.rsqrt(jnp.mean(rows * rows, axis=-1, keepdims=True) + EPS)


def turn(rows, cosine, sine):
    return rows * cosine + pltpu.roll(rows, HEAD // 2, 1) * sine


def dot(a, b):
    return jnp.dot(a, b, preferred_element_type=F32)


def dot_t(a, b):
    return lax.dot_general(a, b, (((1,), (1,)), ((), ())), preferred_element_type=F32)


def split_two(total):
    high = total.astype(BF).astype(F32)
    return high, total - high


def kernel(
    passages, query_weight, kv_weight, out_weight, score_vector, prefix, table,
    owner, row, count, out,
    pas, ends, wq, wkv, wo, pre_v, tab, tail,
    last32, own_rows, own_share, heads_all, pre_keys, req_out, req_in, pick, place,
    last_out, last_in, sums_out, sums_in, query_all, part_out, part_in, slot_last,
    owner_row, row_row, score_v, load_sem, send_sem, recv_sem,
):
    me = lax.axis_index("corpus")
    px = lax.axis_index("pre")

    loads = [
        (owner, owner_row),
        (row, row_row),
        (passages.at[:, pl.ds(16, 16)], ends),
        (query_weight, wq),
        (table.at[pl.ds(PREFIX, TOKENS)], tail),
        (prefix, pre_v),
        (table.at[pl.ds(pl.multiple_of(px * SHARE, SHARE), SHARE)], tab),
        (passages.at[pl.ds(pl.multiple_of(px * BLOCK, BLOCK), BLOCK)], pas),
        (kv_weight, wkv),
        (out_weight, wo),
        (score_vector, score_v),
    ]
    copies = [
        pltpu.make_async_copy(src, dst, load_sem.at[i])
        for i, (src, dst) in enumerate(loads)
    ]

    barrier = pltpu.get_barrier_semaphore()

    def greet(i, carry):
        peer = lax.rem(me + i, OWNERS)
        pl.semaphore_signal(barrier, inc=1, device_id={"corpus": peer}, device_id_type=MESH)
        return carry

    lax.fori_loop(1, OWNERS, greet, 0)
    for k in (2, 1, 3):
        pl.semaphore_signal(
            barrier, inc=1, device_id={"pre": lax.rem(px + k, PRE)}, device_id_type=MESH
        )
    for copy in copies:
        copy.start()

    def spread(source, target, channel):
        def send(i, carry):
            peer = lax.rem(me + i, OWNERS)
            pltpu.make_async_remote_copy(
                src_ref=source.at[peer],
                dst_ref=target.at[me],
                send_sem=send_sem.at[channel],
                recv_sem=recv_sem.at[channel],
                device_id={"corpus": peer},
                device_id_type=MESH,
            ).start()
            return carry

        target[me] = source[me]
        lax.fori_loop(1, OWNERS, send, 0)

    def wait_for(ref, semaphore):
        pltpu.make_async_copy(ref, ref, semaphore).wait()

    copies[0].wait()
    copies[1].wait()
    ia = iota((SLOTS, SLOTS), 0)
    ib = iota((SLOTS, SLOTS), 1)
    owners_r = owner_row[...]
    owners_c = jnp.sum(jnp.where(ia == ib, owners_r.astype(F32), 0.0), axis=1, keepdims=True)
    owners_c = owners_c.astype(jnp.int32)
    same = owners_c == owners_r
    rank_r = jnp.sum(jnp.where(same & (ia < ib), 1.0, 0.0), axis=0, keepdims=True)
    rank_c = jnp.sum(jnp.where(same & (ib < ia), 1.0, 0.0), axis=1, keepdims=True)
    mine = jnp.where(ia == owners_r, row_row[...].astype(F32), 0.0)
    first = jnp.sum(jnp.where(rank_r < 0.5, mine, 0.0), axis=1, keepdims=True)
    second = jnp.sum(jnp.where(rank_r > 0.5, mine, 0.0), axis=1, keepdims=True)
    lane = iota((OWNERS, 128), 1)
    wanted = jnp.where(lane < 8, first, second).astype(jnp.int32)
    wanted = (wanted // BLOCK) * (8 * BLOCK) + (lane & 7) * BLOCK + wanted % BLOCK
    req_out[...] = wanted.astype(F32).reshape(OWNERS, 1, 128)

    spot = owners_c * 16 + rank_c.astype(jnp.int32) * 8
    for j in range(8):
        place[j * SLOTS : (j + 1) * SLOTS, :] = jnp.where(
            iota((SLOTS, OWNERS * 16), 1) == spot + j, 1.0, 0.0
        ).astype(BF)

    copies[2].wait()

    def take_last(r, carry):
        last32[pl.ds(r, 1), :] = ends[r].astype(F32)[15:16, :]
        return carry

    lax.fori_loop(0, PASS, take_last, 0)
    last = last32[...].astype(BF)
    for q in range(PRE):
        for j in range(8):
            start = (q * 8 + j) * BLOCK
            own_rows[start : start + BLOCK, :] = last[
                q * BLOCK : (q + 1) * BLOCK, j * 128 : (j + 1) * 128
            ]

    copies[3].wait()
    copies[4].wait()
    tail_cos, tail_sin = cos_sin(tail[...])
    end_cos, end_sin = tail_cos[TOKENS - 1 :, :], tail_sin[TOKENS - 1 :, :]

    def query_of(normed, g):
        projected = dot(normed, wq[:, 2 * g * HEAD : 2 * (g + 1) * HEAD])
        parts = [
            turn(unit(projected[:, i * HEAD : (i + 1) * HEAD]), end_cos, end_sin).astype(BF)
            for i in range(2)
        ]
        return jnp.concatenate(parts, axis=0)

    copies[5].wait()
    copies[6].wait()
    for half in range(2):
        span = slice(half * 256, (half + 1) * 256)
        cosine, sine = cos_sin(tab[span, :])
        for g in range(GROUPS):
            rows = pre_v[span, g * HEAD : (g + 1) * HEAD].astype(F32)
            keys = turn(unit(rows), cosine, sine).astype(BF)
            if g < WHOLE:
                heads_all[g, px, 0, span, :] = keys
                heads_all[g, px, 1, span, :] = pre_v[
                    span, (GROUPS + g) * HEAD : (GROUPS + g + 1) * HEAD
                ]
            else:
                pre_keys[g, span, :] = keys

    copies[7].wait()
    copies[8].wait()
    hidden = pas[...].reshape(CHUNK, WIDTH)
    hidden32 = hidden.astype(F32)
    factor = lax.rsqrt(jnp.mean(hidden32 * hidden32, axis=-1, keepdims=True) + EPS)
    cosine = jnp.broadcast_to(tail_cos[None], (BLOCK, TOKENS, HEAD)).reshape(CHUNK, HEAD)
    sine = jnp.broadcast_to(tail_sin[None], (BLOCK, TOKENS, HEAD)).reshape(CHUNK, HEAD)
    shape = (2 * BLOCK, CHUNK)
    own = (iota(shape, 0) % BLOCK) == (iota(shape, 1) // TOKENS)
    normed = unit(last32[pl.ds(pl.multiple_of(px * BLOCK, BLOCK), BLOCK), :]).astype(BF)
    for pair in range(GROUPS // 2):
        cols = slice(2 * pair * HEAD, 2 * (pair + 1) * HEAD)
        v_cols = slice((GROUPS + 2 * pair) * HEAD, (GROUPS + 2 * (pair + 1)) * HEAD)
        both_keys = dot(hidden, wkv[:, cols]) * factor
        both_values = (dot(hidden, wkv[:, v_cols]) * factor).astype(BF)
        for i in range(2):
            g = 2 * pair + i
            keys = turn(unit(both_keys[:, i * HEAD : (i + 1) * HEAD]), cosine, sine).astype(BF)
            values = both_values[:, i * HEAD : (i + 1) * HEAD]
            expo = jnp.where(own, jnp.exp(dot_t(query_of(normed, g), keys) * SCALE), 0.0)
            weighted = dot(expo.astype(BF), values).astype(BF)
            high, low = split_two(jnp.sum(expo, axis=1, keepdims=True))
            total = jnp.where(iota((2 * BLOCK, HEAD), 1) < 64, high, low).astype(BF)
            for h in range(2):
                rows = slice(h * BLOCK, (h + 1) * BLOCK)
                own_share[px, 0, 2 * g + h] = weighted[rows]
                own_share[px, 1, 2 * g + h] = total[rows]

    def to_row(ref, channel):
        for k in (2, 1, 3):
            to = lax.rem(px + k, PRE)
            pltpu.make_async_remote_copy(
                src_ref=ref.at[px],
                dst_ref=ref.at[px],
                send_sem=send_sem.at[channel],
                recv_sem=recv_sem.at[channel],
                device_id={"pre": to},
                device_id_type=MESH,
            ).start()

    pl.semaphore_wait(barrier, OWNERS - 1 + PRE - 1)
    spread(req_out, req_in, 0)
    to_row(own_share, 3)
    for g in range(WHOLE):
        to_row(heads_all.at[g], 4 + g)

    wait_for(req_in.at[pl.ds(0, OWNERS - 1)], recv_sem.at[0])
    shape = (OWNERS * 16, 128)
    asked = jnp.broadcast_to(req_in[...], (OWNERS, 16, 128)).reshape(shape)
    asked = jnp.where(iota(shape, 1) == (iota(shape, 0) & 15), asked, 0.0)
    asked = jnp.sum(asked, axis=1, keepdims=True).astype(jnp.int32)
    pick[...] = jnp.where(iota((OWNERS * 16, 8 * PASS), 1) == asked, 1.0, 0.0).astype(BF)
    last_out[...] = dot(pick[...], own_rows[...]).astype(BF).reshape(OWNERS, 16, 128)
    spread(last_out, last_in, 1)
    wait_for(own_share.at[pl.ds(0, PRE - 1)], recv_sem.at[3])
    for i in range(2):
        served = dot(pick[...], own_share[:, i].reshape(HEADS * PASS, HEAD)).astype(BF)
        sums_out[:, i * 16 : (i + 1) * 16, :] = served.reshape(OWNERS, 16, 128)
    spread(sums_out, sums_in, 2)

    wait_for(last_in.at[pl.ds(0, OWNERS - 1)], recv_sem.at[1])
    got = dot(place[...], last_in[...].reshape(OWNERS * 16, 128))
    slot_last[...] = jnp.concatenate(
        [got[j * SLOTS : (j + 1) * SLOTS, :] for j in range(8)], axis=1
    )
    normed = unit(slot_last[...]).astype(BF)
    for g in (*range(WHOLE, GROUPS), *range(WHOLE)):
        query_all[g, px] = query_of(normed, g)
        if g >= WHOLE:
            to_row(query_all.at[g], 4 + g)

    diagonal = iota((HEAD, HEAD), 0) == iota((HEAD, HEAD), 1)
    whole = []
    for g in range(WHOLE):
        wait_for(heads_all.at[g, pl.ds(0, PRE - 1)], recv_sem.at[4 + g])
        weighted = jnp.zeros((2 * SLOTS, HEAD), F32)
        total = jnp.zeros((2 * SLOTS, 1), F32)
        for q in range(PRE):
            expo = jnp.exp(dot_t(query_all[g, px], heads_all[g, q, 0]) * SCALE)
            weighted = weighted + dot(expo.astype(BF), heads_all[g, q, 1])
            total = total + jnp.sum(expo, axis=1, keepdims=True)
        whole.append((weighted, total))
    for g in range(WHOLE, GROUPS):
        wait_for(query_all.at[g, pl.ds(0, PRE - 1)], recv_sem.at[4 + g])
        values = pre_v[:, (GROUPS + g) * HEAD : (GROUPS + g + 1) * HEAD]
        for q in range(PRE):
            expo = jnp.exp(dot_t(query_all[g, q], pre_keys[g]) * SCALE)
            part_out[g, q, 0:HEAD, :] = dot(expo.astype(BF), values).astype(BF)
            total = jnp.sum(expo, axis=1, keepdims=True)
            total = jnp.sum(jnp.where(diagonal, total, 0.0), axis=0, keepdims=True)
            high, low = split_two(total)
            part_out[g, q, HEAD:PART, :] = jnp.where(
                iota((PART - HEAD, HEAD), 0) == 0, high, low
            ).astype(BF)
        part_in[g, px] = part_out[g, px]
        for k in (2, 1, 3):
            to = lax.rem(px + k, PRE)
            pltpu.make_async_remote_copy(
                src_ref=part_out.at[g, to],
                dst_ref=part_in.at[g, px],
                send_sem=send_sem.at[8 + g],
                recv_sem=recv_sem.at[8 + g],
                device_id={"pre": to},
                device_id_type=MESH,
            ).start()

    wait_for(sums_in.at[pl.ds(0, OWNERS - 1)], recv_sem.at[2])
    own_w = dot(place[...], sums_in[:, 0:16, :].reshape(OWNERS * 16, 128))
    own_t = dot(place[...], sums_in[:, 16:32, :].reshape(OWNERS * 16, 128))
    own_t = own_t[:, 0:1] + own_t[:, 64:65]
    copies[9].wait()
    copies[10].wait()
    mixed = []
    for g in range(GROUPS):
        rows = slice(g * 2 * SLOTS, (g + 1) * 2 * SLOTS)
        if g < WHOLE:
            weighted, total = whole[g]
            weighted = weighted + own_w[rows]
        else:
            wait_for(part_in.at[g, pl.ds(0, PRE - 1)], recv_sem.at[8 + g])
            weighted = own_w[rows]
            total = jnp.zeros((1, HEAD), F32)
            for q in range(PRE):
                weighted = weighted + part_in[g, q, 0:HEAD, :].astype(F32)
                sums = part_in[g, q, HEAD:PART, :].astype(F32)
                total = total + sums[0:1, :] + sums[1:2, :]
            total = jnp.sum(jnp.where(diagonal, total, 0.0), axis=1, keepdims=True)
        total = total + own_t[rows]
        result = (weighted / total).astype(BF)
        mixed += [result[0:SLOTS], result[SLOTS:]]
    updated = slot_last[...] + dot(jnp.concatenate(mixed, axis=1), wo[...])
    square = jnp.mean(updated * updated, axis=-1, keepdims=True)
    weights = score_v[...].astype(F32)
    weights = jnp.concatenate([weights[j : j + 1, :] for j in range(8)], axis=1)
    score = jnp.sum(updated * weights, axis=-1, keepdims=True)
    score = score * lax.rsqrt(square + EPS)
    score = jnp.sum(jnp.where(ia == ib, score, 0.0), axis=0, keepdims=True)
    slot = px * SLOTS + iota((1, SLOTS), 1)
    out[...] = jnp.where(slot < count[0], score, 0.0)

    wait_for(req_out.at[pl.ds(0, OWNERS - 1)], send_sem.at[0])
    wait_for(last_out.at[pl.ds(0, OWNERS - 1)], send_sem.at[1])
    wait_for(sums_out.at[pl.ds(0, OWNERS - 1)], send_sem.at[2])
    wait_for(own_share.at[pl.ds(0, PRE - 1)], send_sem.at[3])
    for g in range(WHOLE):
        wait_for(heads_all.at[g, pl.ds(0, PRE - 1)], send_sem.at[4 + g])
    for g in range(WHOLE, GROUPS):
        wait_for(query_all.at[g, pl.ds(0, PRE - 1)], send_sem.at[4 + g])
        wait_for(part_out.at[g, pl.ds(0, PRE - 1)], send_sem.at[8 + g])


def per_device(
    passages,
    query_weight,
    kv_weight,
    out_weight,
    score_vector,
    prefix,
    candidate_owner,
    candidate_row,
    candidate_count,
):
    hbm = pl.BlockSpec(memory_space=pl.ANY)
    return pl.pallas_call(
        kernel,
        out_shape=jax.ShapeDtypeStruct((1, SLOTS), F32),
        in_specs=[hbm] * 9 + [pl.BlockSpec(memory_space=pltpu.SMEM)],
        out_specs=pl.BlockSpec(memory_space=pltpu.VMEM),
        scratch_shapes=[
            pltpu.VMEM((BLOCK, TOKENS, WIDTH), BF),
            pltpu.VMEM((PASS, 16, WIDTH), BF),
            pltpu.VMEM((WIDTH, WIDTH), BF),
            pltpu.VMEM((WIDTH, WIDTH), BF),
            pltpu.VMEM((WIDTH, WIDTH), BF),
            pltpu.VMEM((SHARE, WIDTH), BF),
            pltpu.VMEM((SHARE, HEAD), F32),
            pltpu.VMEM((TOKENS, HEAD), F32),
            pltpu.VMEM((PASS, WIDTH), F32),
            pltpu.VMEM((8 * PASS, 128), BF),
            pltpu.VMEM((PRE, 2, HEADS, BLOCK, HEAD), BF),
            pltpu.VMEM((max(WHOLE, 1), PRE, 2, SHARE, HEAD), BF),
            pltpu.VMEM((GROUPS, SHARE, HEAD), BF),
            pltpu.VMEM((OWNERS, 1, 128), F32),
            pltpu.VMEM((OWNERS, 1, 128), F32),
            pltpu.VMEM((OWNERS * 16, 8 * PASS), BF),
            pltpu.VMEM((8 * SLOTS, OWNERS * 16), BF),
            pltpu.VMEM((OWNERS, 16, 128), BF),
            pltpu.VMEM((OWNERS, 16, 128), BF),
            pltpu.VMEM((OWNERS, 32, 128), BF),
            pltpu.VMEM((OWNERS, 32, 128), BF),
            pltpu.VMEM((GROUPS, PRE, 2 * SLOTS, HEAD), BF),
            pltpu.VMEM((GROUPS, PRE, PART, HEAD), BF),
            pltpu.VMEM((GROUPS, PRE, PART, HEAD), BF),
            pltpu.VMEM((SLOTS, WIDTH), F32),
            pltpu.VMEM((1, SLOTS), jnp.int32),
            pltpu.VMEM((1, SLOTS), jnp.int32),
            pltpu.VMEM((8, 128), BF),
            pltpu.SemaphoreType.DMA((11,)),
            pltpu.SemaphoreType.DMA((12,)),
            pltpu.SemaphoreType.DMA((12,)),
        ],
        compiler_params=pltpu.CompilerParams(
            collective_id=0, has_side_effects=True, vmem_limit_bytes=VLIM * 2**20
        ),
        cost_estimate=pl.CostEstimate(
            flops=6 * 10**9, bytes_accessed=12 * 2**20, transcendentals=2 * 10**6
        ),
    )(
        passages,
        query_weight,
        kv_weight,
        out_weight,
        score_vector.reshape(8, 128),
        prefix[0],
        jnp.asarray(angle_table()),
        candidate_owner.reshape(1, SLOTS),
        candidate_row,
        candidate_count,
    )


def solution(mesh):
    return jax.shard_map(
        per_device,
        mesh=mesh,
        in_specs=(
            P("corpus", None, None),
            P(),
            P(),
            P(),
            P(),
            P("corpus", "pre", None),
            P("corpus", "pre", None),
            P("corpus", "pre"),
            P("corpus"),
        ),
        out_specs=P("corpus", "pre"),
        check_vma=False,
    )
```

```python
import jax
import jax.numpy as jnp
import numpy as np
from jax import lax
from jax.experimental import pallas as pl
from jax.experimental.pallas import tpu as pltpu
from jax.sharding import PartitionSpec as P

MESH = pl.DeviceIdType.MESH
BF = jnp.bfloat16
F32 = jnp.float32

OWNERS = 64
PRE = 4
SLOTS = 64
PASS = 64
TOKENS = 32
WIDTH = 1024
HEADS = 8
GROUPS = 4
HEAD = 128
PREFIX = 2048
SHARE = PREFIX // PRE
CHUNK = 512
SCALE = HEAD**-0.5
EPS = 1e-06
PART = HEAD + 16
VLIM = 62
BLOCK = PASS // PRE
WHOLE = 1


def angle_table():
    half = HEAD // 2
    exponent = np.arange(half, dtype=np.float32) * np.float32(2.0 / HEAD)
    freq = np.float32(1000000.0) ** (-exponent)
    angles = np.arange(PREFIX + TOKENS, dtype=np.float32)[:, None] * freq[None, :]
    angles = angles.astype(np.float64)
    return np.concatenate([np.cos(angles), np.sin(angles)], axis=1).astype(np.float32)


def iota(shape, dim):
    return lax.broadcasted_iota(jnp.int32, shape, dim)


def cos_sin(table):
    swapped = pltpu.roll(table, HEAD // 2, 1)
    low = iota(table.shape, 1) < HEAD // 2
    return jnp.where(low, table, swapped), jnp.where(low, -swapped, table)


def unit(rows):
    return rows * lax.rsqrt(jnp.mean(rows * rows, axis=-1, keepdims=True) + EPS)


def turn(rows, cosine, sine):
    return rows * cosine + pltpu.roll(rows, HEAD // 2, 1) * sine


def dot(a, b):
    return jnp.dot(a, b, preferred_element_type=F32)


def dot_t(a, b):
    return lax.dot_general(a, b, (((1,), (1,)), ((), ())), preferred_element_type=F32)


def split_two(total):
    high = total.astype(BF).astype(F32)
    return high, total - high


def kernel(
    passages, query_weight, kv_weight, out_weight, score_vector, prefix, table,
    owner, row, count, out,
    pas, ends, wq, wkv, wo, pre_v, tab, tail,
    last32, own_rows, own_share, heads_all, pre_keys, req_out, req_in, pick, place,
    last_out, last_in, sums_out, sums_in, query_all, part_out, part_in, slot_last,
    owner_row, row_row, score_v, load_sem, send_sem, recv_sem,
):
    me = lax.axis_index("corpus")
    px = lax.axis_index("pre")

    loads = [
        (owner, owner_row),
        (row, row_row),
        (passages.at[:, pl.ds(16, 16)], ends),
        (query_weight, wq),
        (table.at[pl.ds(PREFIX, TOKENS)], tail),
        (prefix, pre_v),
        (table.at[pl.ds(pl.multiple_of(px * SHARE, SHARE), SHARE)], tab),
        (passages.at[pl.ds(pl.multiple_of(px * BLOCK, BLOCK), BLOCK)], pas),
        (kv_weight, wkv),
        (out_weight, wo),
        (score_vector, score_v),
    ]
    copies = [
        pltpu.make_async_copy(src, dst, load_sem.at[i])
        for i, (src, dst) in enumerate(loads)
    ]

    barrier = pltpu.get_barrier_semaphore()

    def greet(i, carry):
        peer = lax.rem(me + i, OWNERS)
        pl.semaphore_signal(barrier, inc=1, device_id={"corpus": peer}, device_id_type=MESH)
        return carry

    lax.fori_loop(1, OWNERS, greet, 0)
    for k in (2, 1, 3):
        pl.semaphore_signal(
            barrier, inc=1, device_id={"pre": lax.rem(px + k, PRE)}, device_id_type=MESH
        )
    for copy in copies:
        copy.start()

    def spread(source, target, channel):
        def send(i, carry):
            peer = lax.rem(me + i, OWNERS)
            pltpu.make_async_remote_copy(
                src_ref=source.at[peer],
                dst_ref=target.at[me],
                send_sem=send_sem.at[channel],
                recv_sem=recv_sem.at[channel],
                device_id={"corpus": peer},
                device_id_type=MESH,
            ).start()
            return carry

        target[me] = source[me]
        lax.fori_loop(1, OWNERS, send, 0)

    def wait_for(ref, semaphore):
        pltpu.make_async_copy(ref, ref, semaphore).wait()

    copies[0].wait()
    copies[1].wait()
    ia = iota((SLOTS, SLOTS), 0)
    ib = iota((SLOTS, SLOTS), 1)
    owners_r = owner_row[...]
    owners_c = jnp.sum(jnp.where(ia == ib, owners_r.astype(F32), 0.0), axis=1, keepdims=True)
    owners_c = owners_c.astype(jnp.int32)
    same = owners_c == owners_r
    rank_r = jnp.sum(jnp.where(same & (ia < ib), 1.0, 0.0), axis=0, keepdims=True)
    rank_c = jnp.sum(jnp.where(same & (ib < ia), 1.0, 0.0), axis=1, keepdims=True)
    mine = jnp.where(ia == owners_r, row_row[...].astype(F32), 0.0)
    first = jnp.sum(jnp.where(rank_r < 0.5, mine, 0.0), axis=1, keepdims=True)
    second = jnp.sum(jnp.where(rank_r > 0.5, mine, 0.0), axis=1, keepdims=True)
    lane = iota((OWNERS, 128), 1)
    wanted = jnp.where(lane < 8, first, second).astype(jnp.int32)
    wanted = (wanted // BLOCK) * (8 * BLOCK) + (lane & 7) * BLOCK + wanted % BLOCK
    req_out[...] = wanted.astype(F32).reshape(OWNERS, 1, 128)

    spot = owners_c * 16 + rank_c.astype(jnp.int32) * 8
    for j in range(8):
        place[j * SLOTS : (j + 1) * SLOTS, :] = jnp.where(
            iota((SLOTS, OWNERS * 16), 1) == spot + j, 1.0, 0.0
        ).astype(BF)

    copies[2].wait()

    def take_last(r, carry):
        last32[pl.ds(r, 1), :] = ends[r].astype(F32)[15:16, :]
        return carry

    lax.fori_loop(0, PASS, take_last, 0)
    last = last32[...].astype(BF)
    for q in range(PRE):
        for j in range(8):
            start = (q * 8 + j) * BLOCK
            own_rows[start : start + BLOCK, :] = last[
                q * BLOCK : (q + 1) * BLOCK, j * 128 : (j + 1) * 128
            ]

    copies[3].wait()
    copies[4].wait()
    tail_cos, tail_sin = cos_sin(tail[...])
    end_cos, end_sin = tail_cos[TOKENS - 1 :, :], tail_sin[TOKENS - 1 :, :]

    def query_of(normed, g):
        projected = dot(normed, wq[:, 2 * g * HEAD : 2 * (g + 1) * HEAD])
        parts = [
            turn(unit(projected[:, i * HEAD : (i + 1) * HEAD]), end_cos, end_sin).astype(BF)
            for i in range(2)
        ]
        return jnp.concatenate(parts, axis=0)

    def to_row(ref, channel, at=()):
        for k in (2, 1, 3):
            to = lax.rem(px + k, PRE)
            pltpu.make_async_remote_copy(
                src_ref=ref.at[(px, *at)],
                dst_ref=ref.at[(px, *at)],
                send_sem=send_sem.at[channel],
                recv_sem=recv_sem.at[channel],
                device_id={"pre": to},
                device_id_type=MESH,
            ).start()

    copies[5].wait()
    copies[6].wait()

    def prefix_keys(heads):
        for half in range(2):
            span = slice(half * 256, (half + 1) * 256)
            cosine, sine = cos_sin(tab[span, :])
            for g in heads:
                rows = pre_v[span, g * HEAD : (g + 1) * HEAD].astype(F32)
                keys = turn(unit(rows), cosine, sine).astype(BF)
                if g < WHOLE:
                    heads_all[g, px, 0, span, :] = keys
                    heads_all[g, px, 1, span, :] = pre_v[
                        span, (GROUPS + g) * HEAD : (GROUPS + g + 1) * HEAD
                    ]
                else:
                    pre_keys[g, span, :] = keys

    prefix_keys(range(WHOLE))

    pl.semaphore_wait(barrier, OWNERS - 1 + PRE - 1)
    for g in range(WHOLE):
        to_row(heads_all.at[g], 4 + g, (0,))
    spread(req_out, req_in, 0)
    copies[7].wait()
    copies[8].wait()
    hidden = pas[...].reshape(CHUNK, WIDTH)
    hidden32 = hidden.astype(F32)
    factor = lax.rsqrt(jnp.mean(hidden32 * hidden32, axis=-1, keepdims=True) + EPS)
    cosine = jnp.broadcast_to(tail_cos[None], (BLOCK, TOKENS, HEAD)).reshape(CHUNK, HEAD)
    sine = jnp.broadcast_to(tail_sin[None], (BLOCK, TOKENS, HEAD)).reshape(CHUNK, HEAD)
    shape = (2 * BLOCK, CHUNK)
    own = (iota(shape, 0) % BLOCK) == (iota(shape, 1) // TOKENS)
    normed = unit(last32[pl.ds(pl.multiple_of(px * BLOCK, BLOCK), BLOCK), :]).astype(BF)
    for pair in range(GROUPS // 2):
        cols = slice(2 * pair * HEAD, 2 * (pair + 1) * HEAD)
        v_cols = slice((GROUPS + 2 * pair) * HEAD, (GROUPS + 2 * (pair + 1)) * HEAD)
        both_keys = dot(hidden, wkv[:, cols]) * factor
        both_values = (dot(hidden, wkv[:, v_cols]) * factor).astype(BF)
        for i in range(2):
            g = 2 * pair + i
            keys = turn(unit(both_keys[:, i * HEAD : (i + 1) * HEAD]), cosine, sine).astype(BF)
            values = both_values[:, i * HEAD : (i + 1) * HEAD]
            expo = jnp.where(own, jnp.exp(dot_t(query_of(normed, g), keys) * SCALE), 0.0)
            weighted = dot(expo.astype(BF), values).astype(BF)
            high, low = split_two(jnp.sum(expo, axis=1, keepdims=True))
            total = jnp.where(iota((2 * BLOCK, HEAD), 1) < 64, high, low).astype(BF)
            for h in range(2):
                rows = slice(h * BLOCK, (h + 1) * BLOCK)
                own_share[px, 0, 2 * g + h] = weighted[rows]
                own_share[px, 1, 2 * g + h] = total[rows]

    to_row(own_share, 3)
    for g in range(WHOLE):
        to_row(heads_all.at[g], 8 + g, (1,))

    wait_for(req_in.at[pl.ds(0, OWNERS - 1)], recv_sem.at[0])
    shape = (OWNERS * 16, 128)
    asked = jnp.broadcast_to(req_in[...], (OWNERS, 16, 128)).reshape(shape)
    asked = jnp.where(iota(shape, 1) == (iota(shape, 0) & 15), asked, 0.0)
    asked = jnp.sum(asked, axis=1, keepdims=True).astype(jnp.int32)
    pick[...] = jnp.where(iota((OWNERS * 16, 8 * PASS), 1) == asked, 1.0, 0.0).astype(BF)
    last_out[...] = dot(pick[...], own_rows[...]).astype(BF).reshape(OWNERS, 16, 128)
    spread(last_out, last_in, 1)
    prefix_keys(range(WHOLE, GROUPS))
    wait_for(own_share.at[pl.ds(0, PRE - 1)], recv_sem.at[3])
    for i in range(2):
        served = dot(pick[...], own_share[:, i].reshape(HEADS * PASS, HEAD)).astype(BF)
        sums_out[:, i * 16 : (i + 1) * 16, :] = served.reshape(OWNERS, 16, 128)
    spread(sums_out, sums_in, 2)

    wait_for(last_in.at[pl.ds(0, OWNERS - 1)], recv_sem.at[1])
    got = dot(place[...], last_in[...].reshape(OWNERS * 16, 128))
    slot_last[...] = jnp.concatenate(
        [got[j * SLOTS : (j + 1) * SLOTS, :] for j in range(8)], axis=1
    )
    normed = unit(slot_last[...]).astype(BF)
    for g in (*range(WHOLE, GROUPS), *range(WHOLE)):
        query_all[g, px] = query_of(normed, g)
        if g >= WHOLE:
            to_row(query_all.at[g], 4 + g)

    diagonal = iota((HEAD, HEAD), 0) == iota((HEAD, HEAD), 1)
    whole = []
    for g in range(WHOLE):
        wait_for(heads_all.at[g, pl.ds(0, PRE - 1), 0], recv_sem.at[4 + g])
        wait_for(heads_all.at[g, pl.ds(0, PRE - 1), 1], recv_sem.at[8 + g])
        weighted = jnp.zeros((2 * SLOTS, HEAD), F32)
        total = jnp.zeros((2 * SLOTS, 1), F32)
        for q in range(PRE):
            expo = jnp.exp(dot_t(query_all[g, px], heads_all[g, q, 0]) * SCALE)
            weighted = weighted + dot(expo.astype(BF), heads_all[g, q, 1])
            total = total + jnp.sum(expo, axis=1, keepdims=True)
        whole.append((weighted, total))
    for g in range(WHOLE, GROUPS):
        wait_for(query_all.at[g, pl.ds(0, PRE - 1)], recv_sem.at[4 + g])
        values = pre_v[:, (GROUPS + g) * HEAD : (GROUPS + g + 1) * HEAD]
        for q in range(PRE):
            expo = jnp.exp(dot_t(query_all[g, q], pre_keys[g]) * SCALE)
            part_out[g, q, 0:HEAD, :] = dot(expo.astype(BF), values).astype(BF)
            total = jnp.sum(expo, axis=1, keepdims=True)
            total = jnp.sum(jnp.where(diagonal, total, 0.0), axis=0, keepdims=True)
            high, low = split_two(total)
            part_out[g, q, HEAD:PART, :] = jnp.where(
                iota((PART - HEAD, HEAD), 0) == 0, high, low
            ).astype(BF)
        part_in[g, px] = part_out[g, px]
        for k in (2, 1, 3):
            to = lax.rem(px + k, PRE)
            pltpu.make_async_remote_copy(
                src_ref=part_out.at[g, to],
                dst_ref=part_in.at[g, px],
                send_sem=send_sem.at[8 + g],
                recv_sem=recv_sem.at[8 + g],
                device_id={"pre": to},
                device_id_type=MESH,
            ).start()

    wait_for(sums_in.at[pl.ds(0, OWNERS - 1)], recv_sem.at[2])
    own_w = dot(place[...], sums_in[:, 0:16, :].reshape(OWNERS * 16, 128))
    own_t = dot(place[...], sums_in[:, 16:32, :].reshape(OWNERS * 16, 128))
    own_t = own_t[:, 0:1] + own_t[:, 64:65]
    copies[9].wait()
    copies[10].wait()
    mixed = []
    for g in range(GROUPS):
        rows = slice(g * 2 * SLOTS, (g + 1) * 2 * SLOTS)
        if g < WHOLE:
            weighted, total = whole[g]
            weighted = weighted + own_w[rows]
        else:
            wait_for(part_in.at[g, pl.ds(0, PRE - 1)], recv_sem.at[8 + g])
            weighted = own_w[rows]
            total = jnp.zeros((1, HEAD), F32)
            for q in range(PRE):
                weighted = weighted + part_in[g, q, 0:HEAD, :].astype(F32)
                sums = part_in[g, q, HEAD:PART, :].astype(F32)
                total = total + sums[0:1, :] + sums[1:2, :]
            total = jnp.sum(jnp.where(diagonal, total, 0.0), axis=1, keepdims=True)
        total = total + own_t[rows]
        result = (weighted / total).astype(BF)
        mixed += [result[0:SLOTS], result[SLOTS:]]
    updated = slot_last[...] + dot(jnp.concatenate(mixed, axis=1), wo[...])
    square = jnp.mean(updated * updated, axis=-1, keepdims=True)
    weights = score_v[...].astype(F32)
    weights = jnp.concatenate([weights[j : j + 1, :] for j in range(8)], axis=1)
    score = jnp.sum(updated * weights, axis=-1, keepdims=True)
    score = score * lax.rsqrt(square + EPS)
    score = jnp.sum(jnp.where(ia == ib, score, 0.0), axis=0, keepdims=True)
    slot = px * SLOTS + iota((1, SLOTS), 1)
    out[...] = jnp.where(slot < count[0], score, 0.0)

    wait_for(req_out.at[pl.ds(0, OWNERS - 1)], send_sem.at[0])
    wait_for(last_out.at[pl.ds(0, OWNERS - 1)], send_sem.at[1])
    wait_for(sums_out.at[pl.ds(0, OWNERS - 1)], send_sem.at[2])
    wait_for(own_share.at[pl.ds(0, PRE - 1)], send_sem.at[3])
    for g in range(WHOLE):
        wait_for(heads_all.at[g, pl.ds(0, PRE - 1), 0], send_sem.at[4 + g])
        wait_for(heads_all.at[g, pl.ds(0, PRE - 1), 1], send_sem.at[8 + g])
    for g in range(WHOLE, GROUPS):
        wait_for(query_all.at[g, pl.ds(0, PRE - 1)], send_sem.at[4 + g])
        wait_for(part_out.at[g, pl.ds(0, PRE - 1)], send_sem.at[8 + g])


def per_device(
    passages,
    query_weight,
    kv_weight,
    out_weight,
    score_vector,
    prefix,
    candidate_owner,
    candidate_row,
    candidate_count,
):
    hbm = pl.BlockSpec(memory_space=pl.ANY)
    return pl.pallas_call(
        kernel,
        out_shape=jax.ShapeDtypeStruct((1, SLOTS), F32),
        in_specs=[hbm] * 9 + [pl.BlockSpec(memory_space=pltpu.SMEM)],
        out_specs=pl.BlockSpec(memory_space=pltpu.VMEM),
        scratch_shapes=[
            pltpu.VMEM((BLOCK, TOKENS, WIDTH), BF),
            pltpu.VMEM((PASS, 16, WIDTH), BF),
            pltpu.VMEM((WIDTH, WIDTH), BF),
            pltpu.VMEM((WIDTH, WIDTH), BF),
            pltpu.VMEM((WIDTH, WIDTH), BF),
            pltpu.VMEM((SHARE, WIDTH), BF),
            pltpu.VMEM((SHARE, HEAD), F32),
            pltpu.VMEM((TOKENS, HEAD), F32),
            pltpu.VMEM((PASS, WIDTH), F32),
            pltpu.VMEM((8 * PASS, 128), BF),
            pltpu.VMEM((PRE, 2, HEADS, BLOCK, HEAD), BF),
            pltpu.VMEM((max(WHOLE, 1), PRE, 2, SHARE, HEAD), BF),
            pltpu.VMEM((GROUPS, SHARE, HEAD), BF),
            pltpu.VMEM((OWNERS, 1, 128), F32),
            pltpu.VMEM((OWNERS, 1, 128), F32),
            pltpu.VMEM((OWNERS * 16, 8 * PASS), BF),
            pltpu.VMEM((8 * SLOTS, OWNERS * 16), BF),
            pltpu.VMEM((OWNERS, 16, 128), BF),
            pltpu.VMEM((OWNERS, 16, 128), BF),
            pltpu.VMEM((OWNERS, 32, 128), BF),
            pltpu.VMEM((OWNERS, 32, 128), BF),
            pltpu.VMEM((GROUPS, PRE, 2 * SLOTS, HEAD), BF),
            pltpu.VMEM((GROUPS, PRE, PART, HEAD), BF),
            pltpu.VMEM((GROUPS, PRE, PART, HEAD), BF),
            pltpu.VMEM((SLOTS, WIDTH), F32),
            pltpu.VMEM((1, SLOTS), jnp.int32),
            pltpu.VMEM((1, SLOTS), jnp.int32),
            pltpu.VMEM((8, 128), BF),
            pltpu.SemaphoreType.DMA((11,)),
            pltpu.SemaphoreType.DMA((12,)),
            pltpu.SemaphoreType.DMA((12,)),
        ],
        compiler_params=pltpu.CompilerParams(
            collective_id=0, has_side_effects=True, vmem_limit_bytes=VLIM * 2**20
        ),
        cost_estimate=pl.CostEstimate(
            flops=6 * 10**9, bytes_accessed=12 * 2**20, transcendentals=2 * 10**6
        ),
    )(
        passages,
        query_weight,
        kv_weight,
        out_weight,
        score_vector.reshape(8, 128),
        prefix[0],
        jnp.asarray(angle_table()),
        candidate_owner.reshape(1, SLOTS),
        candidate_row,
        candidate_count,
    )


def solution(mesh):
    return jax.shard_map(
        per_device,
        mesh=mesh,
        in_specs=(
            P("corpus", None, None),
            P(),
            P(),
            P(),
            P(),
            P("corpus", "pre", None),
            P("corpus", "pre", None),
            P("corpus", "pre"),
            P("corpus"),
        ),
        out_specs=P("corpus", "pre"),
        check_vma=False,
    )
```

```python
import jax
import jax.numpy as jnp
import numpy as np
from jax import lax
from jax.experimental import pallas as pl
from jax.experimental.pallas import tpu as pltpu
from jax.sharding import PartitionSpec as P

MESH = pl.DeviceIdType.MESH
BF = jnp.bfloat16
F32 = jnp.float32

OWNERS = 64
PRE = 4
SLOTS = 64
PASS = 64
TOKENS = 32
WIDTH = 1024
HEADS = 8
GROUPS = 4
HEAD = 128
PREFIX = 2048
SHARE = PREFIX // PRE
CHUNK = 512
SCALE = HEAD**-0.5
EPS = 1e-06
PART = HEAD + 16
VLIM = 62
BLOCK = PASS // PRE
WHOLE = 1


def angle_table():
    half = HEAD // 2
    exponent = np.arange(half, dtype=np.float32) * np.float32(2.0 / HEAD)
    freq = np.float32(1000000.0) ** (-exponent)
    angles = np.arange(PREFIX + TOKENS, dtype=np.float32)[:, None] * freq[None, :]
    angles = angles.astype(np.float64)
    return np.concatenate([np.cos(angles), np.sin(angles)], axis=1).astype(np.float32)


def iota(shape, dim):
    return lax.broadcasted_iota(jnp.int32, shape, dim)


def cos_sin(table):
    swapped = pltpu.roll(table, HEAD // 2, 1)
    low = iota(table.shape, 1) < HEAD // 2
    return jnp.where(low, table, swapped), jnp.where(low, -swapped, table)


def unit(rows):
    return rows * lax.rsqrt(jnp.mean(rows * rows, axis=-1, keepdims=True) + EPS)


def turn(rows, cosine, sine):
    return rows * cosine + pltpu.roll(rows, HEAD // 2, 1) * sine


def dot(a, b):
    return jnp.dot(a, b, preferred_element_type=F32)


def dot_t(a, b):
    return lax.dot_general(a, b, (((1,), (1,)), ((), ())), preferred_element_type=F32)


def split_two(total):
    high = total.astype(BF).astype(F32)
    return high, total - high


def kernel(
    passages, query_weight, kv_weight, out_weight, score_vector, prefix, table,
    owner, row, count, out,
    pas, ends, wq, wkv, wo, pre_v, tab, tail,
    last32, own_rows, own_query, own_share, heads_all, pre_keys, req_out, req_in, pick, place,
    last_out, last_in, sums_out, sums_in, query_all, part_out, part_in, slot_last,
    tot_out, tot_in, owner_row, row_row, score_v, load_sem, send_sem, recv_sem,
):
    me = lax.axis_index("corpus")
    px = lax.axis_index("pre")

    loads = [
        (owner, owner_row),
        (row, row_row),
        (passages.at[:, pl.ds(16, 16)], ends),
        (query_weight, wq),
        (table.at[pl.ds(PREFIX, TOKENS)], tail),
        (prefix, pre_v),
        (table.at[pl.ds(pl.multiple_of(px * SHARE, SHARE), SHARE)], tab),
        (passages.at[pl.ds(pl.multiple_of(px * BLOCK, BLOCK), BLOCK)], pas),
        (kv_weight, wkv),
        (out_weight, wo),
        (score_vector, score_v),
    ]
    copies = [
        pltpu.make_async_copy(src, dst, load_sem.at[i])
        for i, (src, dst) in enumerate(loads)
    ]

    barrier = pltpu.get_barrier_semaphore()

    def greet(i, carry):
        peer = lax.rem(me + i, OWNERS)
        pl.semaphore_signal(barrier, inc=1, device_id={"corpus": peer}, device_id_type=MESH)
        return carry

    lax.fori_loop(1, OWNERS, greet, 0)
    for k in (2, 1, 3):
        pl.semaphore_signal(
            barrier, inc=1, device_id={"pre": lax.rem(px + k, PRE)}, device_id_type=MESH
        )
    for copy in copies:
        copy.start()

    def spread(source, target, channel):
        def send(i, carry):
            peer = lax.rem(me + i, OWNERS)
            pltpu.make_async_remote_copy(
                src_ref=source.at[peer],
                dst_ref=target.at[me],
                send_sem=send_sem.at[channel],
                recv_sem=recv_sem.at[channel],
                device_id={"corpus": peer},
                device_id_type=MESH,
            ).start()
            return carry

        target[me] = source[me]
        lax.fori_loop(1, OWNERS, send, 0)

    def wait_for(ref, semaphore):
        pltpu.make_async_copy(ref, ref, semaphore).wait()

    copies[0].wait()
    copies[1].wait()
    ia = iota((SLOTS, SLOTS), 0)
    ib = iota((SLOTS, SLOTS), 1)
    owners_r = owner_row[...]
    owners_c = jnp.sum(jnp.where(ia == ib, owners_r.astype(F32), 0.0), axis=1, keepdims=True)
    owners_c = owners_c.astype(jnp.int32)
    same = owners_c == owners_r
    rank_r = jnp.sum(jnp.where(same & (ia < ib), 1.0, 0.0), axis=0, keepdims=True)
    rank_c = jnp.sum(jnp.where(same & (ib < ia), 1.0, 0.0), axis=1, keepdims=True)
    mine = jnp.where(ia == owners_r, row_row[...].astype(F32), 0.0)
    first = jnp.sum(jnp.where(rank_r < 0.5, mine, 0.0), axis=1, keepdims=True)
    second = jnp.sum(jnp.where(rank_r > 0.5, mine, 0.0), axis=1, keepdims=True)
    lane = iota((OWNERS, 128), 1)
    wanted = jnp.where(lane < 8, first, second).astype(jnp.int32)
    wanted = (wanted // BLOCK) * (8 * BLOCK) + (lane & 7) * BLOCK + wanted % BLOCK
    req_out[...] = wanted.astype(F32).reshape(OWNERS, 1, 128)

    spot = owners_c * 16 + rank_c.astype(jnp.int32) * 8
    for j in range(8):
        place[j * SLOTS : (j + 1) * SLOTS, :] = jnp.where(
            iota((SLOTS, OWNERS * 16), 1) == spot + j, 1.0, 0.0
        ).astype(BF)

    copies[2].wait()

    def take_last(r, carry):
        last32[pl.ds(r, 1), :] = ends[r].astype(F32)[15:16, :]
        return carry

    lax.fori_loop(0, PASS, take_last, 0)
    last = last32[...].astype(BF)
    for q in range(PRE):
        for j in range(8):
            start = (q * 8 + j) * BLOCK
            own_rows[start : start + BLOCK, :] = last[
                q * BLOCK : (q + 1) * BLOCK, j * 128 : (j + 1) * 128
            ]

    copies[3].wait()
    copies[4].wait()
    tail_cos, tail_sin = cos_sin(tail[...])
    end_cos, end_sin = tail_cos[TOKENS - 1 :, :], tail_sin[TOKENS - 1 :, :]

    def query_of(normed, g):
        projected = dot(normed, wq[:, 2 * g * HEAD : 2 * (g + 1) * HEAD])
        parts = [
            turn(unit(projected[:, i * HEAD : (i + 1) * HEAD]), end_cos, end_sin).astype(BF)
            for i in range(2)
        ]
        return jnp.concatenate(parts, axis=0)

    normed = unit(last32[pl.ds(pl.multiple_of(px * BLOCK, BLOCK), BLOCK), :]).astype(BF)
    for g in range(GROUPS):
        own_query[g] = query_of(normed, g)

    def to_row(ref, channel, at=()):
        for k in (2, 1, 3):
            to = lax.rem(px + k, PRE)
            pltpu.make_async_remote_copy(
                src_ref=ref.at[(px, *at)],
                dst_ref=ref.at[(px, *at)],
                send_sem=send_sem.at[channel],
                recv_sem=recv_sem.at[channel],
                device_id={"pre": to},
                device_id_type=MESH,
            ).start()

    copies[5].wait()
    copies[6].wait()

    def prefix_keys(heads):
        for half in range(2):
            span = slice(half * 256, (half + 1) * 256)
            cosine, sine = cos_sin(tab[span, :])
            for g in heads:
                rows = pre_v[span, g * HEAD : (g + 1) * HEAD].astype(F32)
                keys = turn(unit(rows), cosine, sine).astype(BF)
                if g < WHOLE:
                    heads_all[g, px, 0, span, :] = keys
                    heads_all[g, px, 1, span, :] = pre_v[
                        span, (GROUPS + g) * HEAD : (GROUPS + g + 1) * HEAD
                    ]
                else:
                    pre_keys[g, span, :] = keys

    prefix_keys(range(WHOLE))

    pl.semaphore_wait(barrier, OWNERS - 1 + PRE - 1)
    for g in range(WHOLE):
        to_row(heads_all.at[g], 4 + g, (0,))
    spread(req_out, req_in, 0)
    copies[7].wait()
    copies[8].wait()
    hidden = pas[...].reshape(CHUNK, WIDTH)
    hidden32 = hidden.astype(F32)
    factor = lax.rsqrt(jnp.mean(hidden32 * hidden32, axis=-1, keepdims=True) + EPS)
    cosine = jnp.broadcast_to(tail_cos[None], (BLOCK, TOKENS, HEAD)).reshape(CHUNK, HEAD)
    sine = jnp.broadcast_to(tail_sin[None], (BLOCK, TOKENS, HEAD)).reshape(CHUNK, HEAD)
    shape = (2 * BLOCK, CHUNK)
    own = (iota(shape, 0) % BLOCK) == (iota(shape, 1) // TOKENS)
    for pair in range(GROUPS // 2):
        cols = slice(2 * pair * HEAD, 2 * (pair + 1) * HEAD)
        v_cols = slice((GROUPS + 2 * pair) * HEAD, (GROUPS + 2 * (pair + 1)) * HEAD)
        both_keys = dot(hidden, wkv[:, cols]) * factor
        both_values = (dot(hidden, wkv[:, v_cols]) * factor).astype(BF)
        for i in range(2):
            g = 2 * pair + i
            keys = turn(unit(both_keys[:, i * HEAD : (i + 1) * HEAD]), cosine, sine).astype(BF)
            values = both_values[:, i * HEAD : (i + 1) * HEAD]
            expo = jnp.where(own, jnp.exp(dot_t(own_query[g], keys) * SCALE), 0.0)
            weighted = dot(expo.astype(BF), values).astype(BF)
            high, low = split_two(jnp.sum(expo, axis=1, keepdims=True))
            total = jnp.where(iota((2 * BLOCK, HEAD), 1) < 64, high, low).astype(BF)
            for h in range(2):
                rows = slice(h * BLOCK, (h + 1) * BLOCK)
                own_share[px, 0, 2 * g + h] = weighted[rows]
                own_share[px, 1, 2 * g + h] = total[rows]

    to_row(own_share, 3)
    for g in range(WHOLE):
        to_row(heads_all.at[g], 8 + g, (1,))

    wait_for(req_in.at[pl.ds(0, OWNERS - 1)], recv_sem.at[0])
    shape = (OWNERS * 16, 128)
    asked = jnp.broadcast_to(req_in[...], (OWNERS, 16, 128)).reshape(shape)
    asked = jnp.where(iota(shape, 1) == (iota(shape, 0) & 15), asked, 0.0)
    asked = jnp.sum(asked, axis=1, keepdims=True).astype(jnp.int32)
    pick[...] = jnp.where(iota((OWNERS * 16, 8 * PASS), 1) == asked, 1.0, 0.0).astype(BF)
    last_out[...] = dot(pick[...], own_rows[...]).astype(BF).reshape(OWNERS, 16, 128)
    spread(last_out, last_in, 1)
    prefix_keys(range(WHOLE, GROUPS))
    wait_for(own_share.at[pl.ds(0, PRE - 1)], recv_sem.at[3])
    shares = [own_share[:, i].reshape(HEADS * PASS, HEAD) for i in range(2)]
    served = dot(pick[...], jnp.concatenate(shares, axis=1))
    sums_out[...] = served[:, 0:128].astype(BF).reshape(OWNERS, 16, 128)
    total = served[:, 128:129] + served[:, 192:193]
    total = jnp.where(iota(shape, 1) == (iota(shape, 0) & 15), total, 0.0)
    tot_out[...] = jnp.sum(total.reshape(OWNERS, 16, 128), axis=1, keepdims=True)
    spread(sums_out, sums_in, 2)

    wait_for(last_in.at[pl.ds(0, OWNERS - 1)], recv_sem.at[1])
    got = dot(place[...], last_in[...].reshape(OWNERS * 16, 128))
    slot_last[...] = jnp.concatenate(
        [got[j * SLOTS : (j + 1) * SLOTS, :] for j in range(8)], axis=1
    )
    normed = unit(slot_last[...]).astype(BF)
    for g in (*range(WHOLE, GROUPS), *range(WHOLE)):
        query_all[g, px] = query_of(normed, g)
        if g >= WHOLE:
            to_row(query_all.at[g], 4 + g)
    spread(tot_out, tot_in, 12)

    diagonal = iota((HEAD, HEAD), 0) == iota((HEAD, HEAD), 1)
    whole = []
    for g in range(WHOLE, GROUPS):
        wait_for(query_all.at[g, pl.ds(0, PRE - 1)], recv_sem.at[4 + g])
        values = pre_v[:, (GROUPS + g) * HEAD : (GROUPS + g + 1) * HEAD]
        for q in range(PRE):
            expo = jnp.exp(dot_t(query_all[g, q], pre_keys[g]) * SCALE)
            part_out[g, q, 0:HEAD, :] = dot(expo.astype(BF), values).astype(BF)
            total = jnp.sum(expo, axis=1, keepdims=True)
            total = jnp.sum(jnp.where(diagonal, total, 0.0), axis=0, keepdims=True)
            high, low = split_two(total)
            part_out[g, q, HEAD:PART, :] = jnp.where(
                iota((PART - HEAD, HEAD), 0) == 0, high, low
            ).astype(BF)
        part_in[g, px] = part_out[g, px]
        for k in (2, 1, 3):
            to = lax.rem(px + k, PRE)
            pltpu.make_async_remote_copy(
                src_ref=part_out.at[g, to],
                dst_ref=part_in.at[g, px],
                send_sem=send_sem.at[8 + g],
                recv_sem=recv_sem.at[8 + g],
                device_id={"pre": to},
                device_id_type=MESH,
            ).start()

    for g in range(WHOLE):
        wait_for(heads_all.at[g, pl.ds(0, PRE - 1), 0], recv_sem.at[4 + g])
        wait_for(heads_all.at[g, pl.ds(0, PRE - 1), 1], recv_sem.at[8 + g])
        weighted = jnp.zeros((2 * SLOTS, HEAD), F32)
        total = jnp.zeros((2 * SLOTS, 1), F32)
        for q in range(PRE):
            expo = jnp.exp(dot_t(query_all[g, px], heads_all[g, q, 0]) * SCALE)
            weighted = weighted + dot(expo.astype(BF), heads_all[g, q, 1])
            total = total + jnp.sum(expo, axis=1, keepdims=True)
        whole.append((weighted, total))
    wait_for(sums_in.at[pl.ds(0, OWNERS - 1)], recv_sem.at[2])
    wait_for(tot_in.at[pl.ds(0, OWNERS - 1)], recv_sem.at[12])
    shape = (OWNERS * 16, 128)
    total = jnp.broadcast_to(tot_in[...], (OWNERS, 16, 128)).reshape(shape)
    total = jnp.where(iota(shape, 1) == (iota(shape, 0) & 15), total, 0.0)
    high, low = split_two(jnp.sum(total, axis=1, keepdims=True))
    total = jnp.where(iota(shape, 1) < 64, high, low).astype(BF)
    got = dot(place[...], jnp.concatenate([sums_in[...].reshape(shape), total], axis=1))
    own_w = got[:, 0:128]
    own_t = got[:, 128:129] + got[:, 192:193]
    copies[9].wait()
    copies[10].wait()
    mixed = []
    for g in range(GROUPS):
        if g == GROUPS - 1:
            part = jnp.concatenate(mixed, axis=1)
            slot_last[...] = slot_last[...] + dot(part, wo[0 : 2 * g * HEAD, :])
            mixed = []
        rows = slice(g * 2 * SLOTS, (g + 1) * 2 * SLOTS)
        if g < WHOLE:
            weighted, total = whole[g]
            weighted = weighted + own_w[rows]
        else:
            wait_for(part_in.at[g, pl.ds(0, PRE - 1)], recv_sem.at[8 + g])
            weighted = own_w[rows]
            total = jnp.zeros((1, HEAD), F32)
            for q in range(PRE):
                weighted = weighted + part_in[g, q, 0:HEAD, :].astype(F32)
                sums = part_in[g, q, HEAD:PART, :].astype(F32)
                total = total + sums[0:1, :] + sums[1:2, :]
            total = jnp.sum(jnp.where(diagonal, total, 0.0), axis=1, keepdims=True)
        total = total + own_t[rows]
        result = (weighted / total).astype(BF)
        mixed += [result[0:SLOTS], result[SLOTS:]]
    part = dot(jnp.concatenate(mixed, axis=1), wo[WIDTH - 2 * HEAD :, :])
    updated = slot_last[...] + part
    square = jnp.mean(updated * updated, axis=-1, keepdims=True)
    weights = score_v[...].astype(F32)
    weights = jnp.concatenate([weights[j : j + 1, :] for j in range(8)], axis=1)
    score = jnp.sum(updated * weights, axis=-1, keepdims=True)
    score = score * lax.rsqrt(square + EPS)
    score = jnp.sum(jnp.where(ia == ib, score, 0.0), axis=0, keepdims=True)
    slot = px * SLOTS + iota((1, SLOTS), 1)
    out[...] = jnp.where(slot < count[0], score, 0.0)

    wait_for(req_out.at[pl.ds(0, OWNERS - 1)], send_sem.at[0])
    wait_for(last_out.at[pl.ds(0, OWNERS - 1)], send_sem.at[1])
    wait_for(sums_out.at[pl.ds(0, OWNERS - 1)], send_sem.at[2])
    wait_for(tot_out.at[pl.ds(0, OWNERS - 1)], send_sem.at[12])
    wait_for(own_share.at[pl.ds(0, PRE - 1)], send_sem.at[3])
    for g in range(WHOLE):
        wait_for(heads_all.at[g, pl.ds(0, PRE - 1), 0], send_sem.at[4 + g])
        wait_for(heads_all.at[g, pl.ds(0, PRE - 1), 1], send_sem.at[8 + g])
    for g in range(WHOLE, GROUPS):
        wait_for(query_all.at[g, pl.ds(0, PRE - 1)], send_sem.at[4 + g])
        wait_for(part_out.at[g, pl.ds(0, PRE - 1)], send_sem.at[8 + g])


def per_device(
    passages,
    query_weight,
    kv_weight,
    out_weight,
    score_vector,
    prefix,
    candidate_owner,
    candidate_row,
    candidate_count,
):
    hbm = pl.BlockSpec(memory_space=pl.ANY)
    return pl.pallas_call(
        kernel,
        out_shape=jax.ShapeDtypeStruct((1, SLOTS), F32),
        in_specs=[hbm] * 9 + [pl.BlockSpec(memory_space=pltpu.SMEM)],
        out_specs=pl.BlockSpec(memory_space=pltpu.VMEM),
        scratch_shapes=[
            pltpu.VMEM((BLOCK, TOKENS, WIDTH), BF),
            pltpu.VMEM((PASS, 16, WIDTH), BF),
            pltpu.VMEM((WIDTH, WIDTH), BF),
            pltpu.VMEM((WIDTH, WIDTH), BF),
            pltpu.VMEM((WIDTH, WIDTH), BF),
            pltpu.VMEM((SHARE, WIDTH), BF),
            pltpu.VMEM((SHARE, HEAD), F32),
            pltpu.VMEM((TOKENS, HEAD), F32),
            pltpu.VMEM((PASS, WIDTH), F32),
            pltpu.VMEM((8 * PASS, 128), BF),
            pltpu.VMEM((GROUPS, 2 * BLOCK, HEAD), BF),
            pltpu.VMEM((PRE, 2, HEADS, BLOCK, HEAD), BF),
            pltpu.VMEM((max(WHOLE, 1), PRE, 2, SHARE, HEAD), BF),
            pltpu.VMEM((GROUPS, SHARE, HEAD), BF),
            pltpu.VMEM((OWNERS, 1, 128), F32),
            pltpu.VMEM((OWNERS, 1, 128), F32),
            pltpu.VMEM((OWNERS * 16, 8 * PASS), BF),
            pltpu.VMEM((8 * SLOTS, OWNERS * 16), BF),
            pltpu.VMEM((OWNERS, 16, 128), BF),
            pltpu.VMEM((OWNERS, 16, 128), BF),
            pltpu.VMEM((OWNERS, 16, 128), BF),
            pltpu.VMEM((OWNERS, 16, 128), BF),
            pltpu.VMEM((GROUPS, PRE, 2 * SLOTS, HEAD), BF),
            pltpu.VMEM((GROUPS, PRE, PART, HEAD), BF),
            pltpu.VMEM((GROUPS, PRE, PART, HEAD), BF),
            pltpu.VMEM((SLOTS, WIDTH), F32),
            pltpu.VMEM((OWNERS, 1, 128), F32),
            pltpu.VMEM((OWNERS, 1, 128), F32),
            pltpu.VMEM((1, SLOTS), jnp.int32),
            pltpu.VMEM((1, SLOTS), jnp.int32),
            pltpu.VMEM((8, 128), BF),
            pltpu.SemaphoreType.DMA((11,)),
            pltpu.SemaphoreType.DMA((13,)),
            pltpu.SemaphoreType.DMA((13,)),
        ],
        compiler_params=pltpu.CompilerParams(
            collective_id=0, has_side_effects=True, vmem_limit_bytes=VLIM * 2**20
        ),
        cost_estimate=pl.CostEstimate(
            flops=6 * 10**9, bytes_accessed=12 * 2**20, transcendentals=2 * 10**6
        ),
    )(
        passages,
        query_weight,
        kv_weight,
        out_weight,
        score_vector.reshape(8, 128),
        prefix[0],
        jnp.asarray(angle_table()),
        candidate_owner.reshape(1, SLOTS),
        candidate_row,
        candidate_count,
    )


def solution(mesh):
    return jax.shard_map(
        per_device,
        mesh=mesh,
        in_specs=(
            P("corpus", None, None),
            P(),
            P(),
            P(),
            P(),
            P("corpus", "pre", None),
            P("corpus", "pre", None),
            P("corpus", "pre"),
            P("corpus"),
        ),
        out_specs=P("corpus", "pre"),
        check_vma=False,
    )
```

```python
import jax
import jax.numpy as jnp
import numpy as np
from jax import lax
from jax.experimental import pallas as pl
from jax.experimental.pallas import tpu as pltpu
from jax.sharding import PartitionSpec as P

MESH = pl.DeviceIdType.MESH
BF = jnp.bfloat16
F32 = jnp.float32

OWNERS = 64
PRE = 4
SLOTS = 64
PASS = 64
TOKENS = 32
WIDTH = 1024
HEADS = 8
GROUPS = 4
HEAD = 128
PREFIX = 2048
SHARE = PREFIX // PRE
CHUNK = 512
SCALE = HEAD**-0.5
EPS = 1e-06
PART = HEAD + 16
VLIM = 62
BLOCK = PASS // PRE
WHOLE = 1


def angle_table():
    half = HEAD // 2
    exponent = np.arange(half, dtype=np.float32) * np.float32(2.0 / HEAD)
    freq = np.float32(1000000.0) ** (-exponent)
    angles = np.arange(PREFIX + TOKENS, dtype=np.float32)[:, None] * freq[None, :]
    angles = angles.astype(np.float64)
    return np.concatenate([np.cos(angles), np.sin(angles)], axis=1).astype(np.float32)


def iota(shape, dim):
    return lax.broadcasted_iota(jnp.int32, shape, dim)


def cos_sin(table):
    swapped = pltpu.roll(table, HEAD // 2, 1)
    low = iota(table.shape, 1) < HEAD // 2
    return jnp.where(low, table, swapped), jnp.where(low, -swapped, table)


def unit(rows):
    return rows * lax.rsqrt(jnp.mean(rows * rows, axis=-1, keepdims=True) + EPS)


def turn(rows, cosine, sine):
    return rows * cosine + pltpu.roll(rows, HEAD // 2, 1) * sine


def dot(a, b):
    return jnp.dot(a, b, preferred_element_type=F32)


def dot_t(a, b):
    return lax.dot_general(a, b, (((1,), (1,)), ((), ())), preferred_element_type=F32)


def split_two(total):
    high = total.astype(BF).astype(F32)
    return high, total - high


def kernel(
    passages, query_weight, kv_weight, out_weight, score_vector, prefix, table,
    owner, row, count, out,
    pas, ends, wq, wkv, wo, pre_v, tab, tail,
    last32, own_rows, own_query, own_share, heads_all, pre_keys, req_out, req_in, pick, place,
    last_out, last_in, sums_out, sums_in, query_all, part_out, part_in, slot_last,
    tot_out, tot_in, owner_row, row_row, score_v, load_sem, send_sem, recv_sem,
):
    me = lax.axis_index("corpus")
    px = lax.axis_index("pre")

    loads = [
        (owner, owner_row),
        (row, row_row),
        (passages.at[:, pl.ds(16, 16)], ends),
        (query_weight, wq),
        (table.at[pl.ds(PREFIX, TOKENS)], tail),
        (prefix, pre_v),
        (table.at[pl.ds(pl.multiple_of(px * SHARE, SHARE), SHARE)], tab),
        (passages.at[pl.ds(pl.multiple_of(px * BLOCK, BLOCK), BLOCK)], pas),
        (kv_weight, wkv),
        (out_weight, wo),
        (score_vector, score_v),
    ]
    copies = [
        pltpu.make_async_copy(src, dst, load_sem.at[i])
        for i, (src, dst) in enumerate(loads)
    ]

    barrier = pltpu.get_barrier_semaphore()

    def greet(i, carry):
        peer = lax.rem(me + i, OWNERS)
        pl.semaphore_signal(barrier, inc=1, device_id={"corpus": peer}, device_id_type=MESH)
        return carry

    lax.fori_loop(1, OWNERS, greet, 0)
    for k in (2, 1, 3):
        pl.semaphore_signal(
            barrier, inc=1, device_id={"pre": lax.rem(px + k, PRE)}, device_id_type=MESH
        )
    for copy in copies:
        copy.start()

    def spread(source, target, channel):
        def send(i, carry):
            peer = lax.rem(me + i, OWNERS)
            pltpu.make_async_remote_copy(
                src_ref=source.at[peer],
                dst_ref=target.at[me],
                send_sem=send_sem.at[channel],
                recv_sem=recv_sem.at[channel],
                device_id={"corpus": peer},
                device_id_type=MESH,
            ).start()
            return carry

        target[me] = source[me]
        lax.fori_loop(1, OWNERS, send, 0)

    def wait_for(ref, semaphore):
        pltpu.make_async_copy(ref, ref, semaphore).wait()

    copies[0].wait()
    copies[1].wait()
    ia = iota((SLOTS, SLOTS), 0)
    ib = iota((SLOTS, SLOTS), 1)
    owners_r = owner_row[...]
    owners_c = jnp.sum(jnp.where(ia == ib, owners_r.astype(F32), 0.0), axis=1, keepdims=True)
    owners_c = owners_c.astype(jnp.int32)
    same = owners_c == owners_r
    rank_r = jnp.sum(jnp.where(same & (ia < ib), 1.0, 0.0), axis=0, keepdims=True)
    rank_c = jnp.sum(jnp.where(same & (ib < ia), 1.0, 0.0), axis=1, keepdims=True)
    mine = jnp.where(ia == owners_r, row_row[...].astype(F32), 0.0)
    first = jnp.sum(jnp.where(rank_r < 0.5, mine, 0.0), axis=1, keepdims=True)
    second = jnp.sum(jnp.where(rank_r > 0.5, mine, 0.0), axis=1, keepdims=True)
    lane = iota((OWNERS, 128), 1)
    wanted = jnp.where(lane < 8, first, second).astype(jnp.int32)
    wanted = (wanted // BLOCK) * (8 * BLOCK) + (lane & 7) * BLOCK + wanted % BLOCK
    req_out[...] = wanted.astype(F32).reshape(OWNERS, 1, 128)

    spot = owners_c * 16 + rank_c.astype(jnp.int32) * 8
    for j in range(8):
        place[j * SLOTS : (j + 1) * SLOTS, :] = jnp.where(
            iota((SLOTS, OWNERS * 16), 1) == spot + j, 1.0, 0.0
        ).astype(BF)

    copies[2].wait()

    def take_last(r, carry):
        last32[pl.ds(r, 1), :] = ends[r].astype(F32)[15:16, :]
        return carry

    lax.fori_loop(0, PASS, take_last, 0)
    last = last32[...].astype(BF)
    for q in range(PRE):
        for j in range(8):
            start = (q * 8 + j) * BLOCK
            own_rows[start : start + BLOCK, :] = last[
                q * BLOCK : (q + 1) * BLOCK, j * 128 : (j + 1) * 128
            ]

    copies[3].wait()
    copies[4].wait()
    tail_cos, tail_sin = cos_sin(tail[...])
    end_cos, end_sin = tail_cos[TOKENS - 1 :, :], tail_sin[TOKENS - 1 :, :]

    def query_of(normed, g):
        projected = dot(normed, wq[:, 2 * g * HEAD : 2 * (g + 1) * HEAD])
        parts = [
            turn(unit(projected[:, i * HEAD : (i + 1) * HEAD]), end_cos, end_sin).astype(BF)
            for i in range(2)
        ]
        return jnp.concatenate(parts, axis=0)

    normed = unit(last32[pl.ds(pl.multiple_of(px * BLOCK, BLOCK), BLOCK), :]).astype(BF)
    for g in range(GROUPS):
        own_query[g] = query_of(normed, g)

    def to_row(ref, channel, at=()):
        for k in (2, 1, 3):
            to = lax.rem(px + k, PRE)
            pltpu.make_async_remote_copy(
                src_ref=ref.at[(px, *at)],
                dst_ref=ref.at[(px, *at)],
                send_sem=send_sem.at[channel],
                recv_sem=recv_sem.at[channel],
                device_id={"pre": to},
                device_id_type=MESH,
            ).start()

    copies[5].wait()
    copies[6].wait()

    def prefix_keys(heads):
        for half in range(2):
            span = slice(half * 256, (half + 1) * 256)
            cosine, sine = cos_sin(tab[span, :])
            for g in heads:
                rows = pre_v[span, g * HEAD : (g + 1) * HEAD].astype(F32)
                keys = turn(unit(rows), cosine, sine).astype(BF)
                if g < WHOLE:
                    heads_all[g, px, 0, span, :] = keys
                    heads_all[g, px, 1, span, :] = pre_v[
                        span, (GROUPS + g) * HEAD : (GROUPS + g + 1) * HEAD
                    ]
                else:
                    pre_keys[g, span, :] = keys

    prefix_keys(range(GROUPS))

    pl.semaphore_wait(barrier, OWNERS - 1 + PRE - 1)
    for g in range(WHOLE):
        to_row(heads_all.at[g], 4 + g, (0,))
    spread(req_out, req_in, 0)
    copies[7].wait()
    copies[8].wait()
    hidden = pas[...].reshape(CHUNK, WIDTH)
    hidden32 = hidden.astype(F32)
    factor = lax.rsqrt(jnp.mean(hidden32 * hidden32, axis=-1, keepdims=True) + EPS)
    cosine = jnp.broadcast_to(tail_cos[None], (BLOCK, TOKENS, HEAD)).reshape(CHUNK, HEAD)
    sine = jnp.broadcast_to(tail_sin[None], (BLOCK, TOKENS, HEAD)).reshape(CHUNK, HEAD)
    shape = (2 * BLOCK, CHUNK)
    own = (iota(shape, 0) % BLOCK) == (iota(shape, 1) // TOKENS)
    for pair in range(GROUPS // 2):
        cols = slice(2 * pair * HEAD, 2 * (pair + 1) * HEAD)
        v_cols = slice((GROUPS + 2 * pair) * HEAD, (GROUPS + 2 * (pair + 1)) * HEAD)
        both_keys = dot(hidden, wkv[:, cols]) * factor
        both_values = (dot(hidden, wkv[:, v_cols]) * factor).astype(BF)
        for i in range(2):
            g = 2 * pair + i
            keys = turn(unit(both_keys[:, i * HEAD : (i + 1) * HEAD]), cosine, sine).astype(BF)
            values = both_values[:, i * HEAD : (i + 1) * HEAD]
            expo = jnp.where(own, jnp.exp(dot_t(own_query[g], keys) * SCALE), 0.0)
            weighted = dot(expo.astype(BF), values).astype(BF)
            high, low = split_two(jnp.sum(expo, axis=1, keepdims=True))
            total = jnp.where(iota((2 * BLOCK, HEAD), 1) < 64, high, low).astype(BF)
            for h in range(2):
                rows = slice(h * BLOCK, (h + 1) * BLOCK)
                own_share[px, 0, 2 * g + h] = weighted[rows]
                own_share[px, 1, 2 * g + h] = total[rows]

    to_row(own_share, 3)
    for g in range(WHOLE):
        to_row(heads_all.at[g], 8 + g, (1,))

    wait_for(req_in.at[pl.ds(0, OWNERS - 1)], recv_sem.at[0])
    shape = (OWNERS * 16, 128)
    asked = jnp.broadcast_to(req_in[...], (OWNERS, 16, 128)).reshape(shape)
    asked = jnp.where(iota(shape, 1) == (iota(shape, 0) & 15), asked, 0.0)
    asked = jnp.sum(asked, axis=1, keepdims=True).astype(jnp.int32)
    pick[...] = jnp.where(iota((OWNERS * 16, 8 * PASS), 1) == asked, 1.0, 0.0).astype(BF)
    last_out[...] = dot(pick[...], own_rows[...]).astype(BF).reshape(OWNERS, 16, 128)
    spread(last_out, last_in, 1)
    wait_for(own_share.at[pl.ds(0, PRE - 1)], recv_sem.at[3])
    shares = [own_share[:, i].reshape(HEADS * PASS, HEAD) for i in range(2)]
    served = dot(pick[...], jnp.concatenate(shares, axis=1))
    sums_out[...] = served[:, 0:128].astype(BF).reshape(OWNERS, 16, 128)
    total = served[:, 128:129] + served[:, 192:193]
    total = jnp.where(iota(shape, 1) == (iota(shape, 0) & 15), total, 0.0)
    tot_out[...] = jnp.sum(total.reshape(OWNERS, 16, 128), axis=1, keepdims=True)
    spread(sums_out, sums_in, 2)

    wait_for(last_in.at[pl.ds(0, OWNERS - 1)], recv_sem.at[1])
    got = dot(place[...], last_in[...].reshape(OWNERS * 16, 128))
    slot_last[...] = jnp.concatenate(
        [got[j * SLOTS : (j + 1) * SLOTS, :] for j in range(8)], axis=1
    )
    normed = unit(slot_last[...]).astype(BF)
    for g in (*range(WHOLE, GROUPS), *range(WHOLE)):
        query_all[g, px] = query_of(normed, g)
        if g >= WHOLE:
            to_row(query_all.at[g], 4 + g)
    spread(tot_out, tot_in, 12)

    diagonal = iota((HEAD, HEAD), 0) == iota((HEAD, HEAD), 1)
    whole = []
    for g in range(WHOLE, GROUPS):
        wait_for(query_all.at[g, pl.ds(0, PRE - 1)], recv_sem.at[4 + g])
        values = pre_v[:, (GROUPS + g) * HEAD : (GROUPS + g + 1) * HEAD]
        for q in range(PRE):
            expo = jnp.exp(dot_t(query_all[g, q], pre_keys[g]) * SCALE)
            part_out[g, q, 0:HEAD, :] = dot(expo.astype(BF), values).astype(BF)
            total = jnp.sum(expo, axis=1, keepdims=True)
            total = jnp.sum(jnp.where(diagonal, total, 0.0), axis=0, keepdims=True)
            high, low = split_two(total)
            part_out[g, q, HEAD:PART, :] = jnp.where(
                iota((PART - HEAD, HEAD), 0) == 0, high, low
            ).astype(BF)
        part_in[g, px] = part_out[g, px]
        for k in (2, 1, 3):
            to = lax.rem(px + k, PRE)
            pltpu.make_async_remote_copy(
                src_ref=part_out.at[g, to],
                dst_ref=part_in.at[g, px],
                send_sem=send_sem.at[8 + g],
                recv_sem=recv_sem.at[8 + g],
                device_id={"pre": to},
                device_id_type=MESH,
            ).start()

    for g in range(WHOLE):
        wait_for(heads_all.at[g, pl.ds(0, PRE - 1), 0], recv_sem.at[4 + g])
        wait_for(heads_all.at[g, pl.ds(0, PRE - 1), 1], recv_sem.at[8 + g])
        weighted = jnp.zeros((2 * SLOTS, HEAD), F32)
        total = jnp.zeros((2 * SLOTS, 1), F32)
        for q in range(PRE):
            expo = jnp.exp(dot_t(query_all[g, px], heads_all[g, q, 0]) * SCALE)
            weighted = weighted + dot(expo.astype(BF), heads_all[g, q, 1])
            total = total + jnp.sum(expo, axis=1, keepdims=True)
        whole.append((weighted, total))
    wait_for(sums_in.at[pl.ds(0, OWNERS - 1)], recv_sem.at[2])
    wait_for(tot_in.at[pl.ds(0, OWNERS - 1)], recv_sem.at[12])
    shape = (OWNERS * 16, 128)
    total = jnp.broadcast_to(tot_in[...], (OWNERS, 16, 128)).reshape(shape)
    total = jnp.where(iota(shape, 1) == (iota(shape, 0) & 15), total, 0.0)
    high, low = split_two(jnp.sum(total, axis=1, keepdims=True))
    total = jnp.where(iota(shape, 1) < 64, high, low).astype(BF)
    got = dot(place[...], jnp.concatenate([sums_in[...].reshape(shape), total], axis=1))
    own_w = got[:, 0:128]
    own_t = got[:, 128:129] + got[:, 192:193]
    copies[9].wait()
    copies[10].wait()
    mixed = []
    for g in range(GROUPS):
        if g == GROUPS - 1:
            part = jnp.concatenate(mixed, axis=1)
            slot_last[...] = slot_last[...] + dot(part, wo[0 : 2 * g * HEAD, :])
            mixed = []
        rows = slice(g * 2 * SLOTS, (g + 1) * 2 * SLOTS)
        if g < WHOLE:
            weighted, total = whole[g]
            weighted = weighted + own_w[rows]
        else:
            wait_for(part_in.at[g, pl.ds(0, PRE - 1)], recv_sem.at[8 + g])
            weighted = own_w[rows]
            total = jnp.zeros((1, HEAD), F32)
            for q in range(PRE):
                weighted = weighted + part_in[g, q, 0:HEAD, :].astype(F32)
                sums = part_in[g, q, HEAD:PART, :].astype(F32)
                total = total + sums[0:1, :] + sums[1:2, :]
            total = jnp.sum(jnp.where(diagonal, total, 0.0), axis=1, keepdims=True)
        total = total + own_t[rows]
        result = (weighted / total).astype(BF)
        mixed += [result[0:SLOTS], result[SLOTS:]]
    part = dot(jnp.concatenate(mixed, axis=1), wo[WIDTH - 2 * HEAD :, :])
    updated = slot_last[...] + part
    square = jnp.mean(updated * updated, axis=-1, keepdims=True)
    weights = score_v[...].astype(F32)
    weights = jnp.concatenate([weights[j : j + 1, :] for j in range(8)], axis=1)
    score = jnp.sum(updated * weights, axis=-1, keepdims=True)
    score = score * lax.rsqrt(square + EPS)
    score = jnp.sum(jnp.where(ia == ib, score, 0.0), axis=0, keepdims=True)
    slot = px * SLOTS + iota((1, SLOTS), 1)
    out[...] = jnp.where(slot < count[0], score, 0.0)

    wait_for(req_out.at[pl.ds(0, OWNERS - 1)], send_sem.at[0])
    wait_for(last_out.at[pl.ds(0, OWNERS - 1)], send_sem.at[1])
    wait_for(sums_out.at[pl.ds(0, OWNERS - 1)], send_sem.at[2])
    wait_for(tot_out.at[pl.ds(0, OWNERS - 1)], send_sem.at[12])
    wait_for(own_share.at[pl.ds(0, PRE - 1)], send_sem.at[3])
    for g in range(WHOLE):
        wait_for(heads_all.at[g, pl.ds(0, PRE - 1), 0], send_sem.at[4 + g])
        wait_for(heads_all.at[g, pl.ds(0, PRE - 1), 1], send_sem.at[8 + g])
    for g in range(WHOLE, GROUPS):
        wait_for(query_all.at[g, pl.ds(0, PRE - 1)], send_sem.at[4 + g])
        wait_for(part_out.at[g, pl.ds(0, PRE - 1)], send_sem.at[8 + g])


def per_device(
    passages,
    query_weight,
    kv_weight,
    out_weight,
    score_vector,
    prefix,
    candidate_owner,
    candidate_row,
    candidate_count,
):
    hbm = pl.BlockSpec(memory_space=pl.ANY)
    return pl.pallas_call(
        kernel,
        out_shape=jax.ShapeDtypeStruct((1, SLOTS), F32),
        in_specs=[hbm] * 9 + [pl.BlockSpec(memory_space=pltpu.SMEM)],
        out_specs=pl.BlockSpec(memory_space=pltpu.VMEM),
        scratch_shapes=[
            pltpu.VMEM((BLOCK, TOKENS, WIDTH), BF),
            pltpu.VMEM((PASS, 16, WIDTH), BF),
            pltpu.VMEM((WIDTH, WIDTH), BF),
            pltpu.VMEM((WIDTH, WIDTH), BF),
            pltpu.VMEM((WIDTH, WIDTH), BF),
            pltpu.VMEM((SHARE, WIDTH), BF),
            pltpu.VMEM((SHARE, HEAD), F32),
            pltpu.VMEM((TOKENS, HEAD), F32),
            pltpu.VMEM((PASS, WIDTH), F32),
            pltpu.VMEM((8 * PASS, 128), BF),
            pltpu.VMEM((GROUPS, 2 * BLOCK, HEAD), BF),
            pltpu.VMEM((PRE, 2, HEADS, BLOCK, HEAD), BF),
            pltpu.VMEM((max(WHOLE, 1), PRE, 2, SHARE, HEAD), BF),
            pltpu.VMEM((GROUPS, SHARE, HEAD), BF),
            pltpu.VMEM((OWNERS, 1, 128), F32),
            pltpu.VMEM((OWNERS, 1, 128), F32),
            pltpu.VMEM((OWNERS * 16, 8 * PASS), BF),
            pltpu.VMEM((8 * SLOTS, OWNERS * 16), BF),
            pltpu.VMEM((OWNERS, 16, 128), BF),
            pltpu.VMEM((OWNERS, 16, 128), BF),
            pltpu.VMEM((OWNERS, 16, 128), BF),
            pltpu.VMEM((OWNERS, 16, 128), BF),
            pltpu.VMEM((GROUPS, PRE, 2 * SLOTS, HEAD), BF),
            pltpu.VMEM((GROUPS, PRE, PART, HEAD), BF),
            pltpu.VMEM((GROUPS, PRE, PART, HEAD), BF),
            pltpu.VMEM((SLOTS, WIDTH), F32),
            pltpu.VMEM((OWNERS, 1, 128), F32),
            pltpu.VMEM((OWNERS, 1, 128), F32),
            pltpu.VMEM((1, SLOTS), jnp.int32),
            pltpu.VMEM((1, SLOTS), jnp.int32),
            pltpu.VMEM((8, 128), BF),
            pltpu.SemaphoreType.DMA((11,)),
            pltpu.SemaphoreType.DMA((13,)),
            pltpu.SemaphoreType.DMA((13,)),
        ],
        compiler_params=pltpu.CompilerParams(
            collective_id=0, has_side_effects=True, vmem_limit_bytes=VLIM * 2**20
        ),
        cost_estimate=pl.CostEstimate(
            flops=6 * 10**9, bytes_accessed=12 * 2**20, transcendentals=2 * 10**6
        ),
    )(
        passages,
        query_weight,
        kv_weight,
        out_weight,
        score_vector.reshape(8, 128),
        prefix[0],
        jnp.asarray(angle_table()),
        candidate_owner.reshape(1, SLOTS),
        candidate_row,
        candidate_count,
    )


def solution(mesh):
    return jax.shard_map(
        per_device,
        mesh=mesh,
        in_specs=(
            P("corpus", None, None),
            P(),
            P(),
            P(),
            P(),
            P("corpus", "pre", None),
            P("corpus", "pre", None),
            P("corpus", "pre"),
            P("corpus"),
        ),
        out_specs=P("corpus", "pre"),
        check_vma=False,
    )
```
